32 devices in a mesh: dom: 8 (over z, x), blk: 4 (over y, core).
Axes of the slice: x: 2, y: 2, z: 4, core: 2. Of those that a mesh axis runs over, the one named last changes fastest.
Arguments:
- degree: int32 [64], P('dom'), may hold values from 1 to 3
- face_elem: int32 [256], P('dom'), may hold values from 0 to 7
- face_side: int32 [256], P('dom'), may hold values from 0 to 8, as said below
- face_peer: int32 [256], P('dom'), may hold values from 0 to 7
- coupling: bfloat16 [256, 320, 320], P('dom', 'blk'), may hold values from -0.078125 to 0.078125
- inv_diag: float32 [64, 320], P('dom', 'blk'), may hold values from 0.5 to 2
- inv_off: bfloat16 [64, 320, 320], P('dom', 'blk'), may hold values from -0.109375 to 0.109375
- source: float32 [64, 320], P('dom', 'blk'), may hold values from -6 to 6
- residual: float32 [64, 320], P('dom', 'blk'), may hold values from -0.6 to 0.6
Outputs:
- adjoint: float32 [64, 320], P('dom', 'blk')
- indicator: float32 [64], P('dom')
The draws below stay inside these ranges and needn't reach their ends.
Inputs may be any that keep to these rules, and one draw needn't show every extreme that they name: `face_side`: among the 32 faces of one partition (aligned blocks of 32 rows) each side from 1 to 8 is named by at least 2 and at most 4 faces, and one side by exactly 4; the remaining faces have side 0.
All inputs are finite; a program needn't handle non-finite values.
Results may differ from the reference program's by a relative error of at most 0.004.
Values may be sent and summed in bfloat16 or wider, within the bound.
A program may use at most 64 MiB of HBM per device.

```python
import math
import jax
import jax.numpy as jnp
from jax import lax

MODES = 64
NU = 320
SWEEPS = 2
NEIGH = 8
E_DEV = 8
F_DEV = 32
CAP = 4
NE = 64
NF = 256
N_DOM = 8


def draw_face_side(key, part):
    first_key = jax.random.fold_in(key, 11)
    second_key = jax.random.fold_in(key, 12)
    third_key = jax.random.fold_in(key, 13)
    lowest = max(1, CAP // 2)
    counts = jax.random.randint(first_key, (N_DOM, NEIGH), lowest, CAP + 1)
    forced = jax.random.randint(second_key, (N_DOM,), 0, NEIGH)
    sides = jnp.arange(NEIGH, dtype=jnp.int32)
    counts = jnp.where(sides[None, :] == forced[:, None], CAP, counts)
    ends = jnp.cumsum(counts, axis=1)
    places = jnp.arange(F_DEV, dtype=jnp.int32)
    label = jnp.sum((places[None, :, None] >= ends[:, None, :]).astype(jnp.int32), axis=2) + 1
    label = jnp.where(places[None, :] < ends[:, -1:], label, 0).astype(jnp.int32)
    shuffle_keys = jax.random.split(third_key, N_DOM)
    shuffled = jax.vmap(jax.random.permutation)(shuffle_keys, label)
    return shuffled.reshape(-1).astype(jnp.int32)


def touch_ends(result, stream_key, smallest, high):
    spot = [jax.random.randint(jax.random.fold_in(stream_key, axis), (), 0, length) for axis, length in enumerate(result.shape)]
    longest = result.shape.index(max(result.shape))
    beside = spot[:longest] + [(spot[longest] + 1) % result.shape[longest]] + spot[longest + 1:]
    return result.at[tuple(spot)].set(smallest).at[tuple(beside)].set(high)


def block_scale(own_key, extent, shards, least, high):
    loudness = 1.0
    for position, parts in shards:
        heights = jax.random.uniform(jax.random.fold_in(jax.random.fold_in(own_key, 6), position), (parts,), jnp.float32, least / len(shards), high / len(shards))
        loudness = loudness * jnp.repeat(jnp.exp(heights), extent[position] // parts).reshape((-1,) + (1,) * (len(extent) - 1 - position))
    return loudness


def normal_values(own_key, shape, width, most, shards=(), held_as=jnp.bfloat16):
    values = jax.random.normal(own_key, shape, jnp.float32) * width
    if len(shards) > 0:
        values = block_scale(own_key, shape, shards, -0.22, 0.18) * values
    return jnp.clip(values, min=-most, max=most).astype(held_as)


def setup_inputs(seed: int = 0) -> dict:
    seeds = jax.random.split(jax.random.key(seed), 10)
    return {
        "degree": touch_ends(jax.random.randint(seeds[0], (NE,), 1, 4), jax.random.fold_in(seeds[0], 1), 1, 3).astype(jnp.int32),
        "face_elem": touch_ends(jax.random.randint(seeds[1], (NF,), 0, E_DEV), jax.random.fold_in(seeds[1], 1), 0, E_DEV - 1).astype(jnp.int32),
        "face_side": draw_face_side(jax.random.fold_in(seeds[9], 71), 0),
        "face_peer": touch_ends(jax.random.randint(seeds[3], (NF,), 0, E_DEV), jax.random.fold_in(seeds[3], 1), 0, E_DEV - 1).astype(jnp.int32),
        "coupling": normal_values(seeds[4], (NF, NU, NU), (16 * NU) ** -0.5, 0.078125, ((0, 8), (1, 4))),
        "inv_diag": jnp.clip(jnp.exp(math.log(2.0) - 1.3862944 * jax.random.uniform(seeds[5], (NE, NU), jnp.float32) ** block_scale(seeds[5], (NE, NU), ((0, 8), (1, 4)), -0.2, 0.2)), 0.5, 2.0),
        "inv_off": normal_values(seeds[6], (NE, NU, NU), (11 * NU) ** -0.5, 0.109375, ((0, 8), (1, 4))),
        "source": normal_values(seeds[7], (NE, NU), 1.0, 6.0, ((0, 8), (1, 4)), jnp.float32),
        "residual": normal_values(seeds[8], (NE, NU), 0.1, 0.6, ((0, 8), (1, 4)), jnp.float32),
    }


def activity(degree):
    limit = (degree + 1) ** 3 * MODES // 64
    modes = jnp.arange(NU, dtype=jnp.int32) % MODES
    return (modes[None, :] < limit[:, None]).astype(jnp.float32)


def apply_inverse(inv_diag, inv_off, values):
    blocks = inv_off.reshape(N_DOM, E_DEV, NU, NU)
    vectors = values.reshape(N_DOM, E_DEV, NU)

    def one_block(item):
        tiles, vecs = item
        return jnp.einsum('eij,ej->ei', tiles.astype(jnp.float32), vecs.astype(jnp.float32))

    product = lax.map(one_block, (blocks, vectors)).reshape(NE, NU)
    return inv_diag * values.astype(jnp.float32) + product


def couple(state_half, coupling, owner, neighbour):
    def step(summed, item):
        tiles, own_ids, peer_ids = item
        tiles_wide = tiles.astype(jnp.float32)
        peer_state = state_half[peer_ids].astype(jnp.float32)
        elem_state = state_half[own_ids].astype(jnp.float32)
        local_terms = jnp.einsum('fij,fj->fi', tiles_wide, peer_state)
        transposed = jnp.einsum('fij,fi->fj', tiles_wide, elem_state)
        summed = summed.at[own_ids].add(local_terms).at[peer_ids].add(transposed)
        return summed, None

    start = jnp.zeros((NE, NU), jnp.float32)
    summed, _ = lax.scan(step, start, (coupling.reshape(N_DOM, F_DEV, NU, NU), owner.reshape(N_DOM, F_DEV), neighbour.reshape(N_DOM, F_DEV)))
    return summed


def reference(degree, face_elem, face_side, face_peer, coupling, inv_diag, inv_off, source, residual):
    mask = activity(degree)
    half_count = NEIGH // 2
    partition = jnp.arange(NF, dtype=jnp.int32) // F_DEV
    offset = jnp.where(face_side == 0, 0, jnp.where(face_side <= half_count, face_side, half_count - face_side)).astype(jnp.int32)
    owner = partition * E_DEV + face_elem
    neighbour = ((partition + offset + N_DOM) % N_DOM) * E_DEV + face_peer
    source_half = (source * mask).astype(jnp.bfloat16)
    base_state = apply_inverse(inv_diag, inv_off, source_half) * mask
    adjoint = base_state
    for sweep_index in range(SWEEPS):
        state_half = adjoint.astype(jnp.bfloat16)
        coupled = couple(state_half, coupling, owner, neighbour)
        coupled_half = (coupled * mask).astype(jnp.bfloat16)
        adjoint = (base_state - apply_inverse(inv_diag, inv_off, coupled_half)) * mask
    indicator = jnp.sum(adjoint * residual * mask, axis=1)
    return adjoint, indicator
```

```python
import functools

import jax
import jax.numpy as jnp
from jax import lax
from jax.experimental import pallas as pl
from jax.experimental.pallas import tpu as pltpu
from jax.sharding import PartitionSpec as P

MODES = 64
SWEEPS = 2
NEIGH = 8
LANES = 128
MESH = pl.DeviceIdType.MESH
NT = (((1,), (1,)), ((), ()))


def slots_of(parts):
    half = NEIGH // 2
    offsets = [0] + list(range(1, half + 1)) + [-k for k in range(1, half + 1)]
    unique, side_slot = [], []
    for offset in offsets:
        wrapped = offset % parts
        if wrapped not in unique:
            unique.append(wrapped)
        side_slot.append(unique.index(wrapped))
    return unique, side_slot


def kernel(
    parts, blocks,
    degree, face_elem, face_side, face_peer, coupling_hbm, inv_diag, inv_off_hbm, source, residual,
    adjoint_out, indicator_out,
    coupling, inv_off, src_buf, state_buf, sent_buf, back_buf, coup_buf, weight_buf,
    load_sem, src_send, src_recv, state_send, state_recv, back_send, back_recv, coup_send, coup_recv,
    weight_send, weight_recv,
):
    unique, side_slot = slots_of(parts)
    slots = len(unique)
    elements, quarter = source.shape
    faces, _, width = coupling.shape
    dom = lax.axis_index("dom")
    blk = lax.axis_index("blk")

    load_inv = pltpu.make_async_copy(inv_off_hbm, inv_off, load_sem.at[0])
    load_coup = pltpu.make_async_copy(coupling_hbm, coupling, load_sem.at[1])
    load_inv.start()
    load_coup.start()

    def siblings():
        return [lax.rem(blk + step, blocks) for step in range(1, blocks)]

    def peers(sign):
        found = []
        for slot in range(slots - 1, 0, -1):
            there = lax.rem(dom + (sign * unique[slot]) % parts, parts)
            found += [(slot, there, k) for k in range(blocks)]
        return found + [(0, dom, k) for k in siblings()]

    barrier = pltpu.get_barrier_semaphore()
    everyone = peers(1)
    for _, there, k in everyone:
        pl.semaphore_signal(barrier, inc=1, device_id=(there, k), device_id_type=MESH)
    pl.semaphore_wait(barrier, len(everyone))

    def send(src, dst, send_sem, recv_sem, there, k):
        pltpu.make_async_remote_copy(
            src_ref=src, dst_ref=dst, send_sem=send_sem, recv_sem=recv_sem,
            device_id=(there, k), device_id_type=MESH,
        ).start()

    def finish(buf, count, sem):
        part = buf.at[pl.ds(0, count)]
        pltpu.make_async_copy(part, part, sem).wait()

    def to_siblings(buf, send_sem, recv_sem):
        for k in siblings():
            send(buf.at[blk], buf.at[blk], send_sem, recv_sem, dom, k)

    def joined(buf, first):
        return jnp.concatenate([buf[first + k][:, :quarter] for k in range(blocks)], axis=1)

    row = lax.broadcasted_iota(jnp.int32, (elements, quarter), 0)
    mode = (lax.broadcasted_iota(jnp.int32, (elements, quarter), 1) + blk * quarter) % MODES
    limit = jnp.zeros((elements, quarter), jnp.int32)
    for e in range(elements):
        step = degree[e] + 1
        limit = jnp.where(row == e, step * step * step * MODES // 64, limit)
    mask = (mode < limit).astype(jnp.float32)

    src_half = (source[...] * mask).astype(jnp.bfloat16).astype(jnp.float32)
    src_buf[blk, :, :quarter] = src_half
    to_siblings(src_buf, src_send, src_recv)

    owner = [face_elem[f] for f in range(faces)]
    target = []
    for f in range(faces):
        side = face_side[f]
        slot = side
        for s, wanted in enumerate(side_slot):
            if wanted != s:
                slot = jnp.where(side == s, wanted, slot)
        target.append(slot * elements + face_peer[f])
    pick_row = lax.broadcasted_iota(jnp.int32, (elements, slots * elements), 0)
    pick_col = lax.broadcasted_iota(jnp.int32, (elements, slots * elements), 1)
    pick = jnp.concatenate(
        [
            jnp.where((pick_row == owner[f]) & (pick_col == target[f]), 1.0, 0.0)
            for f in range(faces)
        ],
        axis=0,
    ).astype(jnp.bfloat16)
    target_row = lax.broadcasted_iota(jnp.int32, (slots * elements, quarter), 0)
    full_row = lax.broadcasted_iota(jnp.int32, (elements, width), 0)

    def invert(own, full):
        total = inv_diag[...] * own
        for e in range(elements):
            left = jnp.where(full_row == e, full, 0.0).astype(jnp.bfloat16)
            total += lax.dot_general(left, inv_off[e], NT, preferred_element_type=jnp.float32)
        return total

    finish(src_buf, blocks - 1, src_recv)
    load_inv.wait()
    base = invert(src_half, joined(src_buf, 0)) * mask
    load_coup.wait()

    adjoint = base
    for sweep in range(SWEEPS):
        state, sent, back, coup = (
            buf.at[sweep] for buf in (state_buf, sent_buf, back_buf, coup_buf)
        )
        own_state = adjoint.astype(jnp.bfloat16).astype(jnp.float32)
        state[blk, :, :quarter] = own_state
        for slot, there, k in peers(-1):
            send(state.at[blk], state.at[slot * blocks + blk],
                 state_send.at[sweep], state_recv.at[sweep], there, k)

        turned = jnp.zeros((slots * elements, width), jnp.float32)
        for f in range(faces):
            line = jnp.sum(jnp.where(row == owner[f], own_state, 0.0), axis=0, keepdims=True)
            left = jnp.where(target_row == target[f], line, 0.0).astype(jnp.bfloat16)
            turned += jnp.dot(left, coupling[f], preferred_element_type=jnp.float32)
        for slot in range(slots):
            for k in range(blocks):
                sent[slot * blocks + k, :, :quarter] = turned[
                    slot * elements:(slot + 1) * elements, k * quarter:(k + 1) * quarter
                ]
        for slot, there, k in peers(1):
            send(sent.at[slot * blocks + k], back.at[slot * blocks + blk],
                 back_send.at[sweep], back_recv.at[sweep], there, k)
        coupled = sent[blk][:, :quarter]

        finish(state, slots * blocks - 1, state_recv.at[sweep])
        every = jnp.concatenate([joined(state, slot * blocks) for slot in range(slots)], axis=0)
        picked = jnp.dot(pick, every.astype(jnp.bfloat16), preferred_element_type=jnp.float32)
        for f in range(faces):
            left = picked[f * elements:(f + 1) * elements].astype(jnp.bfloat16)
            coupled += lax.dot_general(left, coupling[f], NT, preferred_element_type=jnp.float32)

        finish(back, slots * blocks - 1, back_recv.at[sweep])
        for step in range(1, blocks):
            coupled += back[lax.rem(blk + step, blocks)][:, :quarter]
        for place in range(blocks, slots * blocks):
            coupled += back[place][:, :quarter]
        half = (coupled * mask).astype(jnp.bfloat16).astype(jnp.float32)
        coup[blk, :, :quarter] = half
        to_siblings(coup, coup_send.at[sweep], coup_recv.at[sweep])
        finish(coup, blocks - 1, coup_recv.at[sweep])
        adjoint = (base - invert(half, joined(coup, 0))) * mask

    adjoint_out[...] = adjoint
    weights = jnp.sum(adjoint * residual[...] * mask, axis=1, keepdims=True)
    lane = lax.broadcasted_iota(jnp.int32, (elements, LANES), 1)
    sub = lax.broadcasted_iota(jnp.int32, (elements, LANES), 0)
    weight_buf[blk] = jnp.where(lane == sub, weights, 0.0)
    to_siblings(weight_buf, weight_send, weight_recv)
    finish(weight_buf, blocks - 1, weight_recv)
    total = weight_buf[0]
    for k in range(1, blocks):
        total += weight_buf[k]
    indicator_out[...] = jnp.sum(total, axis=0, keepdims=True)[:, :elements]

    finish(src_buf, blocks - 1, src_send)
    finish(weight_buf, blocks - 1, weight_send)
    for sweep in range(SWEEPS):
        finish(state_buf.at[sweep], slots * blocks - 1, state_send.at[sweep])
        finish(back_buf.at[sweep], slots * blocks - 1, back_send.at[sweep])
        finish(coup_buf.at[sweep], blocks - 1, coup_send.at[sweep])


def local(degree, face_elem, face_side, face_peer, coupling, inv_diag, inv_off, source, residual):
    elements, quarter = source.shape
    parts, blocks = lax.axis_size("dom"), lax.axis_size("blk")
    places = len(slots_of(parts)[0]) * blocks
    smem = pl.BlockSpec(memory_space=pltpu.SMEM)
    vmem = pl.BlockSpec(memory_space=pltpu.VMEM)
    hbm = pl.BlockSpec(memory_space=pl.ANY)
    tile = (elements, LANES)
    dma = pltpu.SemaphoreType.DMA
    adjoint, indicator = pl.pallas_call(
        functools.partial(kernel, parts, blocks),
        out_shape=(
            jax.ShapeDtypeStruct((elements, quarter), jnp.float32),
            jax.ShapeDtypeStruct((1, elements), jnp.float32),
        ),
        in_specs=[smem, smem, smem, smem, hbm, vmem, hbm, vmem, vmem],
        out_specs=(vmem, vmem),
        scratch_shapes=[
            pltpu.VMEM(coupling.shape, coupling.dtype),
            pltpu.VMEM(inv_off.shape, inv_off.dtype),
            pltpu.VMEM((blocks,) + tile, jnp.float32),
            pltpu.VMEM((SWEEPS, places) + tile, jnp.float32),
            pltpu.VMEM((SWEEPS, places) + tile, jnp.float32),
            pltpu.VMEM((SWEEPS, places) + tile, jnp.float32),
            pltpu.VMEM((SWEEPS, blocks) + tile, jnp.float32),
            pltpu.VMEM((blocks,) + tile, jnp.float32),
            dma((2,)), dma, dma,
            dma((SWEEPS,)), dma((SWEEPS,)), dma((SWEEPS,)), dma((SWEEPS,)),
            dma((SWEEPS,)), dma((SWEEPS,)),
            dma, dma,
        ],
        compiler_params=pltpu.CompilerParams(
            collective_id=0, has_side_effects=True, vmem_limit_bytes=40 * 2**20
        ),
    )(degree, face_elem, face_side, face_peer, coupling, inv_diag, inv_off, source, residual)
    return adjoint, indicator.reshape(elements)


def solution(mesh):
    in_specs = (
        P("dom"),
        P("dom"),
        P("dom"),
        P("dom"),
        P("dom", "blk", None),
        P("dom", "blk"),
        P("dom", "blk", None),
        P("dom", "blk"),
        P("dom", "blk"),
    )
    out_specs = (P("dom", "blk"), P("dom"))
    return jax.shard_map(local, mesh=mesh, in_specs=in_specs, out_specs=out_specs, check_vma=False)
```

```python
import functools

import jax
import jax.numpy as jnp
from jax import lax
from jax.experimental import pallas as pl
from jax.experimental.pallas import tpu as pltpu
from jax.sharding import PartitionSpec as P

MODES = 64
SWEEPS = 2
NEIGH = 8
LANES = 128
MESH = pl.DeviceIdType.MESH
NT = (((1,), (1,)), ((), ()))


def slots_of(parts):
    half = NEIGH // 2
    offsets = [0] + list(range(1, half + 1)) + [-k for k in range(1, half + 1)]
    unique, side_slot = [], []
    for offset in offsets:
        wrapped = offset % parts
        if wrapped not in unique:
            unique.append(wrapped)
        side_slot.append(unique.index(wrapped))
    return unique, side_slot


def kernel(
    parts, blocks,
    degree_hbm, elem_hbm, side_hbm, peer_hbm, coupling_hbm, diag_hbm, inv_off_hbm, source_hbm,
    residual_hbm,
    adjoint_out, indicator_out,
    degree, face_elem, face_side, face_peer, coupling, inv_diag, inv_off, source, residual,
    src_buf, state_buf, wide_buf, sent_buf, part_buf, out_buf, back_buf, coup_buf, dual_buf,
    load_sem, src_sem, dual_sem, state_sem, wide_sem, part_sem, back_sem, coup_sem,
):
    unique, side_slot = slots_of(parts)
    slots = len(unique)
    elements, quarter = source.shape
    faces, _, width = coupling.shape
    table = slots * elements
    dom = lax.axis_index("dom")
    blk = lax.axis_index("blk")

    loads = [
        pltpu.make_async_copy(src, dst, load_sem.at[place])
        for place, (src, dst) in enumerate([
            (degree_hbm, degree), (source_hbm, source), (elem_hbm, face_elem),
            (side_hbm, face_side), (peer_hbm, face_peer), (diag_hbm, inv_diag),
            (residual_hbm, residual), (inv_off_hbm, inv_off), (coupling_hbm, coupling),
        ])
    ]
    for load in loads:
        load.start()

    siblings = [lax.rem(blk + step, blocks) for step in range(1, blocks)]

    def away(slot, sign):
        return lax.rem(dom + (sign * unique[slot]) % parts, parts)

    barrier = pltpu.get_barrier_semaphore()
    for slot in range(1, slots):
        pl.semaphore_signal(
            barrier, inc=1, device_id=(away(slot, 1), blk), device_id_type=MESH
        )
    for k in siblings:
        pl.semaphore_signal(barrier, inc=1, device_id=(dom, k), device_id_type=MESH)

    def send(src, dst, sems, there, k):
        pltpu.make_async_remote_copy(
            src_ref=src, dst_ref=dst, send_sem=sems.at[0], recv_sem=sems.at[1],
            device_id=(there, k), device_id_type=MESH,
        ).start()

    def finish(buf, count, sem):
        part = buf.at[pl.ds(0, count)]
        pltpu.make_async_copy(part, part, sem).wait()

    def to_siblings(buf, sems):
        for k in siblings:
            send(buf.at[blk], buf.at[blk], sems, dom, k)

    def joined(buf, rows):
        return jnp.concatenate(
            [buf[k][:rows, :quarter].astype(jnp.float32) for k in range(blocks)], axis=1
        )

    row = lax.broadcasted_iota(jnp.int32, (elements, quarter), 0)
    mode = (lax.broadcasted_iota(jnp.int32, (elements, quarter), 1) + blk * quarter) % MODES
    limit = jnp.zeros((elements, quarter), jnp.int32)
    loads[0].wait()
    for e in range(elements):
        step = degree[e] + 1
        limit = jnp.where(row == e, step * step * step * MODES // 64, limit)
    mask = (mode < limit).astype(jnp.float32)
    loads[1].wait()
    src_half = (source[...] * mask).astype(jnp.bfloat16).astype(jnp.float32)
    src_buf[blk, :, :quarter] = src_half

    pl.semaphore_wait(barrier, slots - 1 + blocks - 1)
    to_siblings(src_buf, src_sem)

    for load in loads[2:7]:
        load.wait()
    owner = [face_elem[f] for f in range(faces)]
    target = []
    for f in range(faces):
        side = face_side[f]
        slot = side
        for s, wanted in enumerate(side_slot):
            if wanted != s:
                slot = jnp.where(side == s, wanted, slot)
        target.append(slot * elements + face_peer[f])

    weight = residual[...] * mask
    high = weight.astype(jnp.bfloat16).astype(jnp.float32)
    low = weight - high
    row16 = lax.broadcasted_iota(jnp.int32, (2 * elements, quarter), 0)
    both = jnp.concatenate([high, low], axis=0)
    loads[7].wait()
    dual = jnp.zeros((2 * elements, width), jnp.float32)
    for e in range(elements):
        left = jnp.where((row16 == e) | (row16 == e + elements), both, 0.0).astype(jnp.bfloat16)
        dual += jnp.dot(left, inv_off[e], preferred_element_type=jnp.float32)
    dual = dual[:elements] + dual[elements:]
    own_dual = weight * inv_diag[...]
    own_cols = lax.broadcasted_iota(jnp.int32, (elements, width), 1)
    spread = jnp.concatenate([own_dual] * blocks, axis=1)
    mine = (own_cols >= blk * quarter) & (own_cols < (blk + 1) * quarter)
    dual_buf[blk, :, :width] = dual + jnp.where(mine, spread, 0.0)

    pick_row = lax.broadcasted_iota(jnp.int32, (elements, table), 0)
    pick_col = lax.broadcasted_iota(jnp.int32, (elements, table), 1)
    pick = jnp.concatenate(
        [
            jnp.where((pick_row == owner[f]) & (pick_col == target[f]), 1.0, 0.0)
            for f in range(faces)
        ],
        axis=0,
    ).astype(jnp.bfloat16)
    group = max(1, 256 // quarter)
    starts = list(range(0, faces, group))
    spread_row = lax.broadcasted_iota(jnp.int32, (table, group * elements), 0)
    spread_col = lax.broadcasted_iota(jnp.int32, (table, group * elements), 1)
    place_of = []
    for first in starts:
        hot = jnp.zeros((table, group * elements), jnp.float32)
        for f in range(first, min(first + group, faces)):
            col = (f - first) * elements + owner[f]
            hot = jnp.where((spread_row == target[f]) & (spread_col == col), 1.0, hot)
        place_of.append(hot)
    place_of = jnp.concatenate(place_of, axis=0).astype(jnp.bfloat16)
    group_col = lax.broadcasted_iota(jnp.int32, (elements, group * quarter), 1)
    wide_lane = lax.broadcasted_iota(jnp.int32, (quarter, faces * elements), 1)
    fold_row = lax.broadcasted_iota(jnp.int32, (elements, faces * elements), 0)
    fold_col = lax.broadcasted_iota(jnp.int32, (elements, faces * elements), 1)
    fold = jnp.where(fold_col % elements == fold_row, 1.0, 0.0)
    full_row = lax.broadcasted_iota(jnp.int32, (elements, width), 0)

    def invert(own, full):
        total = inv_diag[...] * own
        for e in range(elements):
            left = jnp.where(full_row == e, full, 0.0).astype(jnp.bfloat16)
            total += lax.dot_general(left, inv_off[e], NT, preferred_element_type=jnp.float32)
        return total

    finish(src_buf, blocks - 1, src_sem.at[1])
    base = invert(src_half, joined(src_buf, elements)) * mask
    loads[8].wait()

    adjoint = base
    for sweep in range(SWEEPS):
        state, wide, sent, part, out, back, coup = (
            buf.at[sweep]
            for buf in (state_buf, wide_buf, sent_buf, part_buf, out_buf, back_buf, coup_buf)
        )
        state_sems, wide_sems, part_sems, back_sems, coup_sems = (
            sems.at[sweep] for sems in (state_sem, wide_sem, part_sem, back_sem, coup_sem)
        )
        own_state = adjoint.astype(jnp.bfloat16).astype(jnp.float32)
        state[0, :, :quarter] = own_state
        for slot in range(1, slots):
            send(state.at[0], state.at[slot], state_sems, away(slot, -1), blk)

        repeated = jnp.concatenate([own_state] * group, axis=1)
        stacked = jnp.concatenate(
            [
                jnp.where(
                    (group_col >= g * quarter) & (group_col < (g + 1) * quarter), repeated, 0.0
                )
                for g in range(group)
            ],
            axis=0,
        ).astype(jnp.bfloat16)
        lefts = jnp.dot(place_of, stacked, preferred_element_type=jnp.float32)
        turned = jnp.zeros((table, width), jnp.float32)
        for index, first in enumerate(starts):
            last = min(first + group, faces)
            depth = (last - first) * quarter
            left = lefts[index * table:(index + 1) * table, :depth].astype(jnp.bfloat16)
            turned += jnp.dot(
                left, coupling[first:last].reshape(depth, width),
                preferred_element_type=jnp.float32,
            )
        for k in range(blocks):
            sent[k, :, :, :quarter] = turned[:, k * quarter:(k + 1) * quarter].reshape(
                slots, elements, quarter
            )
        for k in siblings:
            send(sent.at[k], part.at[blk], part_sems, dom, k)

        if sweep == 0:
            dual_buf[blk, :, width:] = jnp.broadcast_to(
                jnp.sum(weight * base, axis=1, keepdims=True),
                (elements, dual_buf.shape[2] - width),
            )
            to_siblings(dual_buf, dual_sem)

        finish(state, slots - 1, state_sems.at[1])
        column = state[...].reshape(table, LANES)
        if wide.shape[1] > table:
            column = jnp.concatenate(
                [column, jnp.zeros((wide.shape[1] - table, LANES), jnp.float32)], axis=0
            )
        wide[blk] = column.astype(jnp.bfloat16)
        to_siblings(wide, wide_sems)

        finish(part, blocks - 1, part_sems.at[1])
        total = sent[blk]
        for k in siblings:
            total += part[k]
        out[...] = total
        for slot in range(1, slots):
            send(out.at[slot], back.at[slot], back_sems, away(slot, 1), blk)
        coupled = total[0][:, :quarter]

        finish(wide, blocks - 1, wide_sems.at[1])
        every = joined(wide, table).astype(jnp.bfloat16)
        picked = jnp.dot(pick, every, preferred_element_type=jnp.float32).astype(jnp.bfloat16)
        product = lax.dot_general(
            coupling[...].reshape(faces * quarter, width), picked, NT,
            preferred_element_type=jnp.float32,
        )
        held = jnp.zeros((quarter, faces * elements), jnp.float32)
        for f in range(faces):
            chosen = (wide_lane >= f * elements) & (wide_lane < (f + 1) * elements)
            held = jnp.where(chosen, product[f * quarter:(f + 1) * quarter], held)
        coupled += lax.dot_general(
            fold, held, NT, precision=lax.Precision.HIGHEST, preferred_element_type=jnp.float32
        )

        finish(back, slots - 1, back_sems.at[1])
        for slot in range(1, slots):
            coupled += back[slot][:, :quarter]
        half = (coupled * mask).astype(jnp.bfloat16).astype(jnp.float32)
        coup[blk, :, :quarter] = half
        to_siblings(coup, coup_sems)
        finish(coup, blocks - 1, coup_sems.at[1])
        full = joined(coup, elements)
        adjoint = (base - invert(half, full)) * mask

    adjoint_out[...] = adjoint
    finish(dual_buf, blocks - 1, dual_sem.at[1])
    dual = dual_buf[0]
    for k in range(1, blocks):
        dual += dual_buf[k]
    weights = dual[:, width:width + 1] - jnp.sum(dual[:, :width] * full, axis=1, keepdims=True)
    lane = lax.broadcasted_iota(jnp.int32, (elements, elements), 1)
    sub = lax.broadcasted_iota(jnp.int32, (elements, elements), 0)
    indicator_out[...] = jnp.sum(jnp.where(lane == sub, weights, 0.0), axis=0, keepdims=True)

    finish(src_buf, blocks - 1, src_sem.at[0])
    finish(dual_buf, blocks - 1, dual_sem.at[0])
    for sweep in range(SWEEPS):
        finish(state_buf.at[sweep], slots - 1, state_sem.at[sweep, 0])
        finish(wide_buf.at[sweep], blocks - 1, wide_sem.at[sweep, 0])
        finish(part_buf.at[sweep], blocks - 1, part_sem.at[sweep, 0])
        finish(back_buf.at[sweep], slots - 1, back_sem.at[sweep, 0])
        finish(coup_buf.at[sweep], blocks - 1, coup_sem.at[sweep, 0])


def local(degree, face_elem, face_side, face_peer, coupling, inv_diag, inv_off, source, residual):
    elements, quarter = source.shape
    parts, blocks = lax.axis_size("dom"), lax.axis_size("blk")
    width = coupling.shape[2]
    slots = len(slots_of(parts)[0])
    vmem = pl.BlockSpec(memory_space=pltpu.VMEM)
    hbm = pl.BlockSpec(memory_space=pl.ANY)
    tile = (elements, LANES)
    rows = -(-slots * elements // 16) * 16
    dual_width = (width // LANES + 1) * LANES
    dma = pltpu.SemaphoreType.DMA
    args = (degree, face_elem, face_side, face_peer, coupling, inv_diag, inv_off, source, residual)
    adjoint, indicator = pl.pallas_call(
        functools.partial(kernel, parts, blocks),
        out_shape=(
            jax.ShapeDtypeStruct((elements, quarter), jnp.float32),
            jax.ShapeDtypeStruct((1, elements), jnp.float32),
        ),
        in_specs=[hbm] * len(args),
        out_specs=(vmem, vmem),
        scratch_shapes=[pltpu.SMEM(arg.shape, arg.dtype) for arg in args[:4]]
        + [pltpu.VMEM(arg.shape, arg.dtype) for arg in args[4:]]
        + [
            pltpu.VMEM((blocks,) + tile, jnp.float32),
            pltpu.VMEM((SWEEPS, slots) + tile, jnp.float32),
            pltpu.VMEM((SWEEPS, blocks, rows, LANES), jnp.bfloat16),
            pltpu.VMEM((SWEEPS, blocks, slots) + tile, jnp.float32),
            pltpu.VMEM((SWEEPS, blocks, slots) + tile, jnp.float32),
            pltpu.VMEM((SWEEPS, slots) + tile, jnp.float32),
            pltpu.VMEM((SWEEPS, slots) + tile, jnp.float32),
            pltpu.VMEM((SWEEPS, blocks) + tile, jnp.float32),
            pltpu.VMEM((blocks, elements, dual_width), jnp.float32),
            dma((len(args),)), dma((2,)), dma((2,)),
        ]
        + [dma((SWEEPS, 2))] * 5,
        compiler_params=pltpu.CompilerParams(
            collective_id=0, has_side_effects=True, vmem_limit_bytes=60 * 2**20
        ),
    )(*args)
    return adjoint, indicator.reshape(elements)


def solution(mesh):
    in_specs = (
        P("dom"),
        P("dom"),
        P("dom"),
        P("dom"),
        P("dom", "blk", None),
        P("dom", "blk"),
        P("dom", "blk", None),
        P("dom", "blk"),
        P("dom", "blk"),
    )
    out_specs = (P("dom", "blk"), P("dom"))
    return jax.shard_map(local, mesh=mesh, in_specs=in_specs, out_specs=out_specs, check_vma=False)
```

```python
import functools

import jax
import jax.numpy as jnp
from jax import lax
from jax.experimental import pallas as pl
from jax.experimental.pallas import tpu as pltpu
from jax.sharding import PartitionSpec as P

MODES = 64
SWEEPS = 2
NEIGH = 8
LANES = 128
MESH = pl.DeviceIdType.MESH
NT = (((1,), (1,)), ((), ()))


def slots_of(parts):
    half = NEIGH // 2
    offsets = [0] + list(range(1, half + 1)) + [-k for k in range(1, half + 1)]
    unique, side_slot = [], []
    for offset in offsets:
        wrapped = offset % parts
        if wrapped not in unique:
            unique.append(wrapped)
        side_slot.append(unique.index(wrapped))
    return unique, side_slot


def kernel(
    parts, blocks,
    degree_hbm, elem_hbm, side_hbm, peer_hbm, coupling_hbm, diag_hbm, inv_off_hbm, source_hbm,
    residual_hbm,
    result_out,
    degree, face_elem, face_side, face_peer, coupling, inv_diag, inv_off, source, residual,
    src_buf, state_buf, wide_buf, sent_buf, back_buf, coup_buf, dual_buf,
    load_sem, src_sem, dual_sem, state_sem, wide_sem, back_sem, coup_sem,
):
    unique, side_slot = slots_of(parts)
    slots = len(unique)
    elements, quarter = source.shape
    faces, _, width = coupling.shape
    table = slots * elements
    dom = lax.axis_index("dom")
    blk = lax.axis_index("blk")

    loads = [
        pltpu.make_async_copy(src, dst, load_sem.at[place])
        for place, (src, dst) in enumerate([
            (degree_hbm, degree), (source_hbm, source), (elem_hbm, face_elem),
            (side_hbm, face_side), (peer_hbm, face_peer), (diag_hbm, inv_diag),
            (residual_hbm, residual), (inv_off_hbm, inv_off), (coupling_hbm, coupling),
        ])
    ]
    for load in loads:
        load.start()

    siblings = [lax.rem(blk + step, blocks) for step in range(1, blocks)]

    def away(slot, sign):
        return lax.rem(dom + (sign * unique[slot]) % parts, parts)

    barrier = pltpu.get_barrier_semaphore()
    for slot in range(1, slots):
        pl.semaphore_signal(
            barrier, inc=1, device_id=(away(slot, 1), blk), device_id_type=MESH
        )
    for k in siblings:
        pl.semaphore_signal(barrier, inc=1, device_id=(dom, k), device_id_type=MESH)

    def send(src, dst, sems, there, k):
        pltpu.make_async_remote_copy(
            src_ref=src, dst_ref=dst, send_sem=sems.at[0], recv_sem=sems.at[1],
            device_id=(there, k), device_id_type=MESH,
        ).start()

    def finish(buf, count, sem):
        part = buf.at[pl.ds(0, count)]
        pltpu.make_async_copy(part, part, sem).wait()

    def to_siblings(buf, sems):
        for k in siblings:
            send(buf.at[blk], buf.at[blk], sems, dom, k)

    def joined(buf, rows):
        return jnp.concatenate(
            [buf[k][:rows, :quarter].astype(jnp.float32) for k in range(blocks)], axis=1
        )

    row = lax.broadcasted_iota(jnp.int32, (elements, quarter), 0)
    mode = (lax.broadcasted_iota(jnp.int32, (elements, quarter), 1) + blk * quarter) % MODES
    full_row = lax.broadcasted_iota(jnp.int32, (elements, width), 0)
    full_col = lax.broadcasted_iota(jnp.int32, (elements, width), 1)
    mine = (full_col >= blk * quarter) & (full_col < (blk + 1) * quarter)

    def in_place(values):
        return jnp.where(mine, jnp.concatenate([values] * blocks, axis=1), 0.0)

    def own_part(values):
        found = values[:, :quarter]
        for k in range(1, blocks):
            found = jnp.where(blk == k, values[:, k * quarter:(k + 1) * quarter], found)
        return found

    limit = jnp.zeros((elements, quarter), jnp.int32)
    full_limit = jnp.zeros((elements, width), jnp.int32)
    loads[0].wait()
    for e in range(elements):
        step = degree[e] + 1
        count = step * step * step * MODES // 64
        limit = jnp.where(row == e, count, limit)
        full_limit = jnp.where(full_row == e, count, full_limit)
    mask = (mode < limit).astype(jnp.float32)
    full_mask = (full_col % MODES < full_limit).astype(jnp.float32)
    loads[1].wait()
    src_half = (source[...] * mask).astype(jnp.bfloat16).astype(jnp.float32)
    src_buf[blk, :, :quarter] = src_half

    pl.semaphore_wait(barrier, slots - 1 + blocks - 1)
    to_siblings(src_buf, src_sem)

    for load in loads[2:7]:
        load.wait()
    owner = [face_elem[f] for f in range(faces)]
    target = []
    for f in range(faces):
        side = face_side[f]
        slot = side
        for s, wanted in enumerate(side_slot):
            if wanted != s:
                slot = jnp.where(side == s, wanted, slot)
        target.append(slot * elements + face_peer[f])

    weight = residual[...] * mask
    high = weight.astype(jnp.bfloat16).astype(jnp.float32)
    low = weight - high
    row16 = lax.broadcasted_iota(jnp.int32, (2 * elements, quarter), 0)
    both = jnp.concatenate([high, low], axis=0)
    loads[7].wait()
    dual = jnp.zeros((2 * elements, width), jnp.float32)
    for e in range(elements):
        left = jnp.where((row16 == e) | (row16 == e + elements), both, 0.0).astype(jnp.bfloat16)
        dual += jnp.dot(left, inv_off[e], preferred_element_type=jnp.float32)
    dual = dual[:elements] + dual[elements:]
    dual_buf[blk, :, :width] = dual + in_place(weight * inv_diag[...])

    pick_row = lax.broadcasted_iota(jnp.int32, (elements, table), 0)
    pick_col = lax.broadcasted_iota(jnp.int32, (elements, table), 1)
    pick = jnp.concatenate(
        [
            jnp.where((pick_row == owner[f]) & (pick_col == target[f]), 1.0, 0.0)
            for f in range(faces)
        ],
        axis=0,
    ).astype(jnp.bfloat16)
    group = max(1, 256 // quarter)
    starts = list(range(0, faces, group))
    spread_row = lax.broadcasted_iota(jnp.int32, (table, group * elements), 0)
    spread_col = lax.broadcasted_iota(jnp.int32, (table, group * elements), 1)
    place_of = []
    for first in starts:
        hot = jnp.zeros((table, group * elements), jnp.float32)
        for f in range(first, min(first + group, faces)):
            col = (f - first) * elements + owner[f]
            hot = jnp.where((spread_row == target[f]) & (spread_col == col), 1.0, hot)
        place_of.append(hot)
    place_of = jnp.concatenate(place_of, axis=0).astype(jnp.bfloat16)
    group_col = lax.broadcasted_iota(jnp.int32, (elements, group * quarter), 1)
    wide_lane = lax.broadcasted_iota(jnp.int32, (quarter, faces * elements), 1)
    fold_row = lax.broadcasted_iota(jnp.int32, (elements, faces * elements), 0)
    fold_col = lax.broadcasted_iota(jnp.int32, (elements, faces * elements), 1)
    fold = jnp.where(fold_col % elements == fold_row, 1.0, 0.0)

    def invert(own, full):
        total = inv_diag[...] * own
        for e in range(elements):
            left = jnp.where(full_row == e, full, 0.0).astype(jnp.bfloat16)
            total += lax.dot_general(left, inv_off[e], NT, preferred_element_type=jnp.float32)
        return total

    finish(src_buf, blocks - 1, src_sem.at[1])
    base = invert(src_half, joined(src_buf, elements)) * mask
    dual_buf[blk, :, width:] = jnp.broadcast_to(
        jnp.sum(weight * base, axis=1, keepdims=True), (elements, dual_buf.shape[2] - width)
    )
    loads[8].wait()

    def one_sweep(sweep, carry):
        adjoint, _ = carry
        state, wide, sent, back, coup = (
            buf.at[sweep] for buf in (state_buf, wide_buf, sent_buf, back_buf, coup_buf)
        )
        state_sems, wide_sems, back_sems, coup_sems = (
            sems.at[sweep] for sems in (state_sem, wide_sem, back_sem, coup_sem)
        )
        own_state = adjoint.astype(jnp.bfloat16).astype(jnp.float32)
        state[0, :, :quarter] = own_state
        for slot in range(1, slots):
            send(state.at[0], state.at[slot], state_sems, away(slot, -1), blk)

        repeated = jnp.concatenate([own_state] * group, axis=1)
        stacked = jnp.concatenate(
            [
                jnp.where(
                    (group_col >= g * quarter) & (group_col < (g + 1) * quarter), repeated, 0.0
                )
                for g in range(group)
            ],
            axis=0,
        ).astype(jnp.bfloat16)
        lefts = jnp.dot(place_of, stacked, preferred_element_type=jnp.float32)
        turned = jnp.zeros((table, width), jnp.float32)
        for index, first in enumerate(starts):
            last = min(first + group, faces)
            depth = (last - first) * quarter
            left = lefts[index * table:(index + 1) * table, :depth].astype(jnp.bfloat16)
            turned += jnp.dot(
                left, coupling[first:last].reshape(depth, width),
                preferred_element_type=jnp.float32,
            )
        sent[:, :, :width] = turned.reshape(slots, elements, width)
        for slot in range(1, slots):
            send(sent.at[slot], back.at[slot], back_sems, away(slot, 1), blk)

        finish(state, slots - 1, state_sems.at[1])
        column = state[...].reshape(table, LANES)
        if wide.shape[1] > table:
            column = jnp.concatenate(
                [column, jnp.zeros((wide.shape[1] - table, LANES), jnp.float32)], axis=0
            )
        wide[blk] = column.astype(jnp.bfloat16)
        to_siblings(wide, wide_sems)

        finish(wide, blocks - 1, wide_sems.at[1])
        every = joined(wide, table).astype(jnp.bfloat16)
        picked = jnp.dot(pick, every, preferred_element_type=jnp.float32).astype(jnp.bfloat16)
        product = lax.dot_general(
            coupling[...].reshape(faces * quarter, width), picked, NT,
            preferred_element_type=jnp.float32,
        )
        held = jnp.zeros((quarter, faces * elements), jnp.float32)
        for f in range(faces):
            chosen = (wide_lane >= f * elements) & (wide_lane < (f + 1) * elements)
            held = jnp.where(chosen, product[f * quarter:(f + 1) * quarter], held)
        own_terms = lax.dot_general(
            fold, held, NT, precision=lax.Precision.HIGHEST, preferred_element_type=jnp.float32
        )
        partial = turned[:elements] + in_place(own_terms)

        finish(back, slots - 1, back_sems.at[1])
        for slot in range(1, slots):
            partial += back[slot][:, :width]
        coup[blk, :, :width] = partial
        to_siblings(coup, coup_sems)
        finish(coup, blocks - 1, coup_sems.at[1])
        coupled = coup[0]
        for k in range(1, blocks):
            coupled += coup[k]
        full = (coupled[:, :width] * full_mask).astype(jnp.bfloat16).astype(jnp.float32)
        return (base - invert(own_part(full), full)) * mask, full

    to_siblings(dual_buf, dual_sem)
    adjoint, full = lax.fori_loop(
        0, SWEEPS, one_sweep, (base, jnp.zeros((elements, width), jnp.float32))
    )

    result_out[:elements, :quarter] = adjoint
    finish(dual_buf, blocks - 1, dual_sem.at[1])
    dual = dual_buf[0]
    for k in range(1, blocks):
        dual += dual_buf[k]
    weights = dual[:, width:width + 1] - jnp.sum(dual[:, :width] * full, axis=1, keepdims=True)
    lane = lax.broadcasted_iota(jnp.int32, (elements, LANES), 1)
    sub = lax.broadcasted_iota(jnp.int32, (elements, LANES), 0)
    result_out[elements:elements + 1, :] = jnp.sum(
        jnp.where(lane == sub, weights, 0.0), axis=0, keepdims=True
    )

    finish(src_buf, blocks - 1, src_sem.at[0])
    finish(dual_buf, blocks - 1, dual_sem.at[0])
    for sweep in range(SWEEPS):
        finish(state_buf.at[sweep], slots - 1, state_sem.at[sweep, 0])
        finish(wide_buf.at[sweep], blocks - 1, wide_sem.at[sweep, 0])
        finish(back_buf.at[sweep], slots - 1, back_sem.at[sweep, 0])
        finish(coup_buf.at[sweep], blocks - 1, coup_sem.at[sweep, 0])


def local(degree, face_elem, face_side, face_peer, coupling, inv_diag, inv_off, source, residual):
    elements, quarter = source.shape
    parts, blocks = lax.axis_size("dom"), lax.axis_size("blk")
    width = coupling.shape[2]
    slots = len(slots_of(parts)[0])
    vmem = pl.BlockSpec(memory_space=pltpu.VMEM)
    hbm = pl.BlockSpec(memory_space=pl.ANY)
    tile = (elements, LANES)
    rows = -(-slots * elements // 16) * 16
    dual_width = (width // LANES + 1) * LANES
    full_width = -(-width // LANES) * LANES
    dma = pltpu.SemaphoreType.DMA
    args = (degree, face_elem, face_side, face_peer, coupling, inv_diag, inv_off, source, residual)
    result = pl.pallas_call(
        functools.partial(kernel, parts, blocks),
        out_shape=jax.ShapeDtypeStruct((2 * elements, LANES), jnp.float32),
        in_specs=[hbm] * len(args),
        out_specs=vmem,
        scratch_shapes=[pltpu.SMEM(arg.shape, arg.dtype) for arg in args[:4]]
        + [pltpu.VMEM(arg.shape, arg.dtype) for arg in args[4:]]
        + [
            pltpu.VMEM((blocks,) + tile, jnp.float32),
            pltpu.VMEM((SWEEPS, slots) + tile, jnp.float32),
            pltpu.VMEM((SWEEPS, blocks, rows, LANES), jnp.bfloat16),
            pltpu.VMEM((SWEEPS, slots, elements, full_width), jnp.float32),
            pltpu.VMEM((SWEEPS, slots, elements, full_width), jnp.float32),
            pltpu.VMEM((SWEEPS, blocks, elements, full_width), jnp.float32),
            pltpu.VMEM((blocks, elements, dual_width), jnp.float32),
            dma((len(args),)), dma((2,)), dma((2,)),
        ]
        + [dma((SWEEPS, 2))] * 4,
        compiler_params=pltpu.CompilerParams(
            collective_id=0, has_side_effects=True, vmem_limit_bytes=60 * 2**20
        ),
    )(*args)
    return result[:elements, :quarter], result[elements, :elements]


def solution(mesh):
    in_specs = (
        P("dom"),
        P("dom"),
        P("dom"),
        P("dom"),
        P("dom", "blk", None),
        P("dom", "blk"),
        P("dom", "blk", None),
        P("dom", "blk"),
        P("dom", "blk"),
    )
    out_specs = (P("dom", "blk"), P("dom"))
    return jax.shard_map(local, mesh=mesh, in_specs=in_specs, out_specs=out_specs, check_vma=False)
```

```python
import functools
import math

import jax
import jax.numpy as jnp
from jax import lax
from jax.experimental import pallas as pl
from jax.experimental.pallas import tpu as pltpu
from jax.sharding import PartitionSpec as P

MODES = 64
SWEEPS = 2
NEIGH = 8
LANES = 128
MESH = pl.DeviceIdType.MESH
NT = (((1,), (1,)), ((), ()))


def slots_of(parts):
    half = NEIGH // 2
    offsets = [0] + list(range(1, half + 1)) + [-k for k in range(1, half + 1)]
    unique, side_slot = [], []
    for offset in offsets:
        wrapped = offset % parts
        if wrapped not in unique:
            unique.append(wrapped)
        side_slot.append(unique.index(wrapped))
    return unique, side_slot


def kernel(
    parts, blocks,
    degree_hbm, elem_hbm, side_hbm, peer_hbm, coupling_hbm, diag_hbm, inv_off_hbm, source_hbm,
    residual_hbm,
    result_out,
    degree, face_elem, face_side, face_peer, coupling, inv_diag, inv_off, source, residual,
    src_buf, state_buf, sent_buf, back_buf, coup_buf, dual_buf,
    load_sem, src_sem, dual_sem, state_sem, back_sem, coup_sem,
):
    unique, side_slot = slots_of(parts)
    slots = len(unique)
    elements, quarter = source.shape
    faces, _, width = coupling.shape
    table = slots * elements
    dom = lax.axis_index("dom")
    blk = lax.axis_index("blk")

    loads = [
        pltpu.make_async_copy(src, dst, load_sem.at[place])
        for place, (src, dst) in enumerate([
            (degree_hbm, degree), (source_hbm, source), (elem_hbm, face_elem),
            (side_hbm, face_side), (peer_hbm, face_peer), (diag_hbm, inv_diag),
            (residual_hbm, residual), (inv_off_hbm, inv_off), (coupling_hbm, coupling),
        ])
    ]
    for load in loads:
        load.start()

    siblings = [lax.rem(blk + step, blocks) for step in range(1, blocks)]

    def away(slot, sign):
        return lax.rem(dom + (sign * unique[slot]) % parts, parts)

    barrier = pltpu.get_barrier_semaphore()
    for slot in range(1, slots):
        for k in range(blocks):
            pl.semaphore_signal(
                barrier, inc=1, device_id=(away(slot, 1), k), device_id_type=MESH
            )
    for k in siblings:
        pl.semaphore_signal(barrier, inc=1, device_id=(dom, k), device_id_type=MESH)

    def send(src, dst, sems, there, k):
        pltpu.make_async_remote_copy(
            src_ref=src, dst_ref=dst, send_sem=sems.at[0], recv_sem=sems.at[1],
            device_id=(there, k), device_id_type=MESH,
        ).start()

    def finish(buf, count, sem):
        part = buf.at[pl.ds(0, count)]
        pltpu.make_async_copy(part, part, sem).wait()

    def to_siblings(buf, sems):
        for k in siblings:
            send(buf.at[blk], buf.at[blk], sems, dom, k)

    def joined(buf, rows):
        return jnp.concatenate(
            [buf[k][:rows, :quarter].astype(jnp.float32) for k in range(blocks)], axis=1
        )

    row = lax.broadcasted_iota(jnp.int32, (elements, quarter), 0)
    mode = (lax.broadcasted_iota(jnp.int32, (elements, quarter), 1) + blk * quarter) % MODES
    full_row = lax.broadcasted_iota(jnp.int32, (elements, width), 0)
    full_col = lax.broadcasted_iota(jnp.int32, (elements, width), 1)
    mine = (full_col >= blk * quarter) & (full_col < (blk + 1) * quarter)

    def in_place(values):
        return jnp.where(mine, jnp.concatenate([values] * blocks, axis=1), 0.0)

    def own_part(values):
        found = values[:, :quarter]
        for k in range(1, blocks):
            found = jnp.where(blk == k, values[:, k * quarter:(k + 1) * quarter], found)
        return found

    limit = jnp.zeros((elements, quarter), jnp.int32)
    full_limit = jnp.zeros((elements, width), jnp.int32)
    loads[0].wait()
    for e in range(elements):
        step = degree[e] + 1
        count = step * step * step * MODES // 64
        limit = jnp.where(row == e, count, limit)
        full_limit = jnp.where(full_row == e, count, full_limit)
    mask = (mode < limit).astype(jnp.float32)
    full_mask = (full_col % MODES < full_limit).astype(jnp.float32)
    loads[1].wait()
    src_half = (source[...] * mask).astype(jnp.bfloat16).astype(jnp.float32)
    src_buf[blk, :, :quarter] = src_half

    pl.semaphore_wait(barrier, slots * blocks - 1)
    to_siblings(src_buf, src_sem)

    for load in loads[2:7]:
        load.wait()
    owner = [face_elem[f] for f in range(faces)]
    target = []
    for f in range(faces):
        side = face_side[f]
        slot = side
        for s, wanted in enumerate(side_slot):
            if wanted != s:
                slot = jnp.where(side == s, wanted, slot)
        target.append(slot * elements + face_peer[f])

    weight = residual[...] * mask
    high = weight.astype(jnp.bfloat16).astype(jnp.float32)
    low = weight - high
    row16 = lax.broadcasted_iota(jnp.int32, (2 * elements, quarter), 0)
    both = jnp.concatenate([high, low], axis=0)
    loads[7].wait()
    dual = jnp.zeros((2 * elements, width), jnp.float32)
    for e in range(elements):
        left = jnp.where((row16 == e) | (row16 == e + elements), both, 0.0).astype(jnp.bfloat16)
        dual += jnp.dot(left, inv_off[e], preferred_element_type=jnp.float32)
    dual = dual[:elements] + dual[elements:]
    dual_buf[blk, :, :width] = dual + in_place(weight * inv_diag[...])

    pick_row = lax.broadcasted_iota(jnp.int32, (elements, table), 0)
    pick_col = lax.broadcasted_iota(jnp.int32, (elements, table), 1)
    pick = jnp.concatenate(
        [
            jnp.where((pick_row == owner[f]) & (pick_col == target[f]), 1.0, 0.0)
            for f in range(faces)
        ],
        axis=0,
    ).astype(jnp.bfloat16)
    group = max(1, 256 // quarter)
    starts = list(range(0, faces, group))
    spread_row = lax.broadcasted_iota(jnp.int32, (table, group * elements), 0)
    spread_col = lax.broadcasted_iota(jnp.int32, (table, group * elements), 1)
    place_of = []
    for first in starts:
        hot = jnp.zeros((table, group * elements), jnp.float32)
        for f in range(first, min(first + group, faces)):
            col = (f - first) * elements + owner[f]
            hot = jnp.where((spread_row == target[f]) & (spread_col == col), 1.0, hot)
        place_of.append(hot)
    place_of = jnp.concatenate(place_of, axis=0).astype(jnp.bfloat16)
    group_col = lax.broadcasted_iota(jnp.int32, (elements, group * quarter), 1)
    chunk = math.gcd(faces, max(1, LANES // elements))
    chunk_lane = lax.broadcasted_iota(jnp.int32, (quarter, chunk * elements), 1)
    fold_row = lax.broadcasted_iota(jnp.int32, (elements, 2 * chunk * elements), 0)
    fold_col = lax.broadcasted_iota(jnp.int32, (elements, 2 * chunk * elements), 1)
    fold = jnp.where(fold_col % elements == fold_row, 1.0, 0.0).astype(jnp.bfloat16)

    def invert(own, full):
        total = inv_diag[...] * own
        for e in range(elements):
            left = jnp.where(full_row == e, full, 0.0).astype(jnp.bfloat16)
            total += lax.dot_general(left, inv_off[e], NT, preferred_element_type=jnp.float32)
        return total

    finish(src_buf, blocks - 1, src_sem.at[1])
    base = invert(src_half, joined(src_buf, elements)) * mask
    dual_buf[blk, :, width:] = jnp.broadcast_to(
        jnp.sum(weight * base, axis=1, keepdims=True), (elements, dual_buf.shape[2] - width)
    )
    loads[8].wait()

    def one_sweep(sweep, carry):
        adjoint, _ = carry
        state, sent, back, coup = (
            buf.at[sweep] for buf in (state_buf, sent_buf, back_buf, coup_buf)
        )
        state_sems, back_sems, coup_sems = (
            sems.at[sweep] for sems in (state_sem, back_sem, coup_sem)
        )
        own_state = adjoint.astype(jnp.bfloat16).astype(jnp.float32)
        state[blk] = jnp.concatenate(
            [own_state, jnp.zeros((elements, LANES - quarter), jnp.float32)], axis=1
        ).astype(jnp.bfloat16)
        for slot in range(1, slots):
            for k in range(blocks):
                send(state.at[blk], state.at[slot * blocks + blk], state_sems, away(slot, -1), k)
        to_siblings(state, state_sems)

        repeated = jnp.concatenate([own_state] * group, axis=1)
        stacked = jnp.concatenate(
            [
                jnp.where(
                    (group_col >= g * quarter) & (group_col < (g + 1) * quarter), repeated, 0.0
                )
                for g in range(group)
            ],
            axis=0,
        ).astype(jnp.bfloat16)
        lefts = jnp.dot(place_of, stacked, preferred_element_type=jnp.float32)
        turned = jnp.zeros((table, width), jnp.float32)
        for index, first in enumerate(starts):
            last = min(first + group, faces)
            depth = (last - first) * quarter
            left = lefts[index * table:(index + 1) * table, :depth].astype(jnp.bfloat16)
            turned += jnp.dot(
                left, coupling[first:last].reshape(depth, width),
                preferred_element_type=jnp.float32,
            )
        sent[:, :, :width] = turned.reshape(slots, elements, width)
        for slot in range(1, slots):
            send(sent.at[slot], back.at[slot], back_sems, away(slot, 1), blk)

        finish(state, slots * blocks - 1, state_sems.at[1])
        every = jnp.concatenate(
            [
                jnp.concatenate(
                    [
                        state[slot * blocks + k].astype(jnp.float32)[:, :quarter]
                        for k in range(blocks)
                    ],
                    axis=1,
                )
                for slot in range(slots)
            ],
            axis=0,
        ).astype(jnp.bfloat16)
        picked = jnp.dot(pick, every, preferred_element_type=jnp.float32).astype(jnp.bfloat16)
        held = jnp.zeros((quarter, chunk * elements), jnp.float32)
        for first in range(0, faces, chunk):
            product = lax.dot_general(
                coupling[first:first + chunk].reshape(chunk * quarter, width),
                picked[first * elements:(first + chunk) * elements],
                NT,
                preferred_element_type=jnp.float32,
            )
            for f in range(chunk):
                chosen = (chunk_lane >= f * elements) & (chunk_lane < (f + 1) * elements)
                held += jnp.where(chosen, product[f * quarter:(f + 1) * quarter], 0.0)
        high = held.astype(jnp.bfloat16)
        low = (held - high.astype(jnp.float32)).astype(jnp.bfloat16)
        own_terms = lax.dot_general(
            fold, jnp.concatenate([high, low], axis=1), NT, preferred_element_type=jnp.float32
        )
        partial = turned[:elements] + in_place(own_terms)

        finish(back, slots - 1, back_sems.at[1])
        for slot in range(1, slots):
            partial += back[slot][:, :width]
        coup[blk, :, :width] = partial
        to_siblings(coup, coup_sems)
        finish(coup, blocks - 1, coup_sems.at[1])
        coupled = coup[0]
        for k in range(1, blocks):
            coupled += coup[k]
        full = (coupled[:, :width] * full_mask).astype(jnp.bfloat16).astype(jnp.float32)
        return (base - invert(own_part(full), full)) * mask, full

    to_siblings(dual_buf, dual_sem)
    adjoint, full = lax.fori_loop(
        0, SWEEPS, one_sweep, (base, jnp.zeros((elements, width), jnp.float32))
    )

    result_out[:elements, :quarter] = adjoint
    finish(dual_buf, blocks - 1, dual_sem.at[1])
    dual = dual_buf[0]
    for k in range(1, blocks):
        dual += dual_buf[k]
    weights = dual[:, width:width + 1] - jnp.sum(dual[:, :width] * full, axis=1, keepdims=True)
    lane = lax.broadcasted_iota(jnp.int32, (elements, LANES), 1)
    sub = lax.broadcasted_iota(jnp.int32, (elements, LANES), 0)
    result_out[elements:elements + 1, :] = jnp.sum(
        jnp.where(lane == sub, weights, 0.0), axis=0, keepdims=True
    )

    finish(src_buf, blocks - 1, src_sem.at[0])
    finish(dual_buf, blocks - 1, dual_sem.at[0])
    for sweep in range(SWEEPS):
        finish(state_buf.at[sweep], slots * blocks - 1, state_sem.at[sweep, 0])
        finish(back_buf.at[sweep], slots - 1, back_sem.at[sweep, 0])
        finish(coup_buf.at[sweep], blocks - 1, coup_sem.at[sweep, 0])


def split_result(result, adjoint, indicator):
    elements, quarter = adjoint.shape
    adjoint[...] = result[:elements, :quarter]
    indicator[...] = result[elements:elements + 1, :elements]


def local(degree, face_elem, face_side, face_peer, coupling, inv_diag, inv_off, source, residual):
    elements, quarter = source.shape
    parts, blocks = lax.axis_size("dom"), lax.axis_size("blk")
    width = coupling.shape[2]
    slots = len(slots_of(parts)[0])
    vmem = pl.BlockSpec(memory_space=pltpu.VMEM)
    hbm = pl.BlockSpec(memory_space=pl.ANY)
    tile = (elements, LANES)
    dual_width = (width // LANES + 1) * LANES
    full_width = -(-width // LANES) * LANES
    dma = pltpu.SemaphoreType.DMA
    args = (degree, face_elem, face_side, face_peer, coupling, inv_diag, inv_off, source, residual)
    result = pl.pallas_call(
        functools.partial(kernel, parts, blocks),
        out_shape=jax.ShapeDtypeStruct((2 * elements, LANES), jnp.float32),
        in_specs=[hbm] * len(args),
        out_specs=vmem,
        scratch_shapes=[pltpu.SMEM(arg.shape, arg.dtype) for arg in args[:4]]
        + [pltpu.VMEM(arg.shape, arg.dtype) for arg in args[4:]]
        + [
            pltpu.VMEM((blocks,) + tile, jnp.float32),
            pltpu.VMEM((SWEEPS, slots * blocks) + tile, jnp.bfloat16),
            pltpu.VMEM((SWEEPS, slots, elements, full_width), jnp.float32),
            pltpu.VMEM((SWEEPS, slots, elements, full_width), jnp.float32),
            pltpu.VMEM((SWEEPS, blocks, elements, full_width), jnp.float32),
            pltpu.VMEM((blocks, elements, dual_width), jnp.float32),
            dma((len(args),)), dma((2,)), dma((2,)),
        ]
        + [dma((SWEEPS, 2))] * 3,
        compiler_params=pltpu.CompilerParams(
            collective_id=0, has_side_effects=True, vmem_limit_bytes=60 * 2**20
        ),
    )(*args)
    adjoint, indicator = pl.pallas_call(
        split_result,
        out_shape=(
            jax.ShapeDtypeStruct((elements, quarter), jnp.float32),
            jax.ShapeDtypeStruct((1, elements), jnp.float32),
        ),
        in_specs=[vmem],
        out_specs=(vmem, vmem),
    )(result)
    return adjoint, indicator.reshape(elements)


def solution(mesh):
    in_specs = (
        P("dom"),
        P("dom"),
        P("dom"),
        P("dom"),
        P("dom", "blk", None),
        P("dom", "blk"),
        P("dom", "blk", None),
        P("dom", "blk"),
        P("dom", "blk"),
    )
    out_specs = (P("dom", "blk"), P("dom"))
    return jax.shard_map(local, mesh=mesh, in_specs=in_specs, out_specs=out_specs, check_vma=False)
```

```python
import functools
import math

import jax
import jax.numpy as jnp
from jax import lax
from jax.experimental import pallas as pl
from jax.experimental.pallas import tpu as pltpu
from jax.sharding import PartitionSpec as P

MODES = 64
SWEEPS = 2
NEIGH = 8
LANES = 128
MESH = pl.DeviceIdType.MESH
NT = (((1,), (1,)), ((), ()))


def slots_of(parts):
    half = NEIGH // 2
    offsets = [0] + list(range(1, half + 1)) + [-k for k in range(1, half + 1)]
    unique, side_slot = [], []
    for offset in offsets:
        wrapped = offset % parts
        if wrapped not in unique:
            unique.append(wrapped)
        side_slot.append(unique.index(wrapped))
    return unique, side_slot


def kernel(
    parts, blocks,
    degree_hbm, elem_hbm, side_hbm, peer_hbm, coupling_hbm, diag_hbm, inv_off_hbm, source_hbm,
    residual_hbm,
    result_out,
    degree, face_elem, face_side, face_peer, coupling, inv_diag, inv_off, source, residual,
    src_buf, state_buf, sent_buf, back_buf, coup_buf, dual_buf,
    load_sem, src_sem, dual_sem, state_sem, back_sem, coup_sem,
):
    unique, side_slot = slots_of(parts)
    slots = len(unique)
    elements, quarter = source.shape
    faces, _, width = coupling.shape
    table = slots * elements
    dom = lax.axis_index("dom")
    blk = lax.axis_index("blk")

    loads = [
        pltpu.make_async_copy(src, dst, load_sem.at[place])
        for place, (src, dst) in enumerate([
            (degree_hbm, degree), (source_hbm, source), (elem_hbm, face_elem),
            (side_hbm, face_side), (peer_hbm, face_peer), (diag_hbm, inv_diag),
            (residual_hbm, residual), (inv_off_hbm, inv_off), (coupling_hbm, coupling),
        ])
    ]
    for load in loads:
        load.start()

    siblings = [lax.rem(blk + step, blocks) for step in range(1, blocks)]

    def away(slot, sign):
        return lax.rem(dom + (sign * unique[slot]) % parts, parts)

    barrier = pltpu.get_barrier_semaphore()
    for slot in range(1, slots):
        for k in range(blocks):
            pl.semaphore_signal(
                barrier, inc=1, device_id=(away(slot, 1), k), device_id_type=MESH
            )
    for k in siblings:
        pl.semaphore_signal(barrier, inc=1, device_id=(dom, k), device_id_type=MESH)

    def send(src, dst, sems, there, k):
        pltpu.make_async_remote_copy(
            src_ref=src, dst_ref=dst, send_sem=sems.at[0], recv_sem=sems.at[1],
            device_id=(there, k), device_id_type=MESH,
        ).start()

    def finish(buf, count, sem):
        part = buf.at[pl.ds(0, count)]
        pltpu.make_async_copy(part, part, sem).wait()

    def to_siblings(buf, sems):
        for k in siblings:
            send(buf.at[blk], buf.at[blk], sems, dom, k)

    def joined(buf, rows):
        return jnp.concatenate(
            [buf[k][:rows, :quarter].astype(jnp.float32) for k in range(blocks)], axis=1
        )

    row = lax.broadcasted_iota(jnp.int32, (elements, quarter), 0)
    mode = (lax.broadcasted_iota(jnp.int32, (elements, quarter), 1) + blk * quarter) % MODES
    full_row = lax.broadcasted_iota(jnp.int32, (elements, width), 0)
    full_col = lax.broadcasted_iota(jnp.int32, (elements, width), 1)
    mine = (full_col >= blk * quarter) & (full_col < (blk + 1) * quarter)

    def in_place(values):
        return jnp.where(mine, jnp.concatenate([values] * blocks, axis=1), 0.0)

    def own_part(values):
        found = values[:, :quarter]
        for k in range(1, blocks):
            found = jnp.where(blk == k, values[:, k * quarter:(k + 1) * quarter], found)
        return found

    limit = jnp.zeros((elements, quarter), jnp.int32)
    full_limit = jnp.zeros((elements, width), jnp.int32)
    loads[0].wait()
    for e in range(elements):
        step = degree[e] + 1
        count = step * step * step * MODES // 64
        limit = jnp.where(row == e, count, limit)
        full_limit = jnp.where(full_row == e, count, full_limit)
    mask = (mode < limit).astype(jnp.float32)
    full_mask = (full_col % MODES < full_limit).astype(jnp.float32)
    loads[1].wait()
    src_half = (source[...] * mask).astype(jnp.bfloat16).astype(jnp.float32)
    src_buf[blk, :, :quarter] = src_half

    for load in loads[2:7]:
        load.wait()
    owner = [face_elem[f] for f in range(faces)]
    target = []
    for f in range(faces):
        side = face_side[f]
        slot = side
        for s, wanted in enumerate(side_slot):
            if wanted != s:
                slot = jnp.where(side == s, wanted, slot)
        target.append(slot * elements + face_peer[f])

    pick_row = lax.broadcasted_iota(jnp.int32, (elements, table), 0)
    pick_col = lax.broadcasted_iota(jnp.int32, (elements, table), 1)
    pick = jnp.concatenate(
        [
            jnp.where((pick_row == owner[f]) & (pick_col == target[f]), 1.0, 0.0)
            for f in range(faces)
        ],
        axis=0,
    ).astype(jnp.bfloat16)
    group = max(1, 256 // quarter)
    starts = list(range(0, faces, group))
    spread_row = lax.broadcasted_iota(jnp.int32, (table, group * elements), 0)
    spread_col = lax.broadcasted_iota(jnp.int32, (table, group * elements), 1)
    place_of = []
    for first in starts:
        hot = jnp.zeros((table, group * elements), jnp.float32)
        for f in range(first, min(first + group, faces)):
            col = (f - first) * elements + owner[f]
            hot = jnp.where((spread_row == target[f]) & (spread_col == col), 1.0, hot)
        place_of.append(hot)
    place_of = jnp.concatenate(place_of, axis=0).astype(jnp.bfloat16)
    group_col = lax.broadcasted_iota(jnp.int32, (elements, group * quarter), 1)
    chunk = math.gcd(faces, max(1, LANES // elements))
    chunk_lane = lax.broadcasted_iota(jnp.int32, (quarter, chunk * elements), 1)
    fold_row = lax.broadcasted_iota(jnp.int32, (elements, 2 * chunk * elements), 0)
    fold_col = lax.broadcasted_iota(jnp.int32, (elements, 2 * chunk * elements), 1)
    fold = jnp.where(fold_col % elements == fold_row, 1.0, 0.0).astype(jnp.bfloat16)

    pl.semaphore_wait(barrier, slots * blocks - 1)
    to_siblings(src_buf, src_sem)

    weight = residual[...] * mask
    high = weight.astype(jnp.bfloat16).astype(jnp.float32)
    low = weight - high
    row16 = lax.broadcasted_iota(jnp.int32, (2 * elements, quarter), 0)
    both = jnp.concatenate([high, low], axis=0)
    loads[7].wait()
    dual = jnp.zeros((2 * elements, width), jnp.float32)
    for e in range(elements):
        left = jnp.where((row16 == e) | (row16 == e + elements), both, 0.0).astype(jnp.bfloat16)
        dual += jnp.dot(left, inv_off[e], preferred_element_type=jnp.float32)
    dual = dual[:elements] + dual[elements:]
    dual_buf[blk, :, :width] = dual + in_place(weight * inv_diag[...])

    def invert(own, full):
        total = inv_diag[...] * own
        for e in range(elements):
            left = jnp.where(full_row == e, full, 0.0).astype(jnp.bfloat16)
            total += lax.dot_general(left, inv_off[e], NT, preferred_element_type=jnp.float32)
        return total

    finish(src_buf, blocks - 1, src_sem.at[1])
    base = invert(src_half, joined(src_buf, elements)) * mask
    dual_buf[blk, :, width:] = jnp.broadcast_to(
        jnp.sum(weight * base, axis=1, keepdims=True), (elements, dual_buf.shape[2] - width)
    )
    loads[8].wait()

    def one_sweep(sweep, carry):
        adjoint, _ = carry
        state, sent, back, coup = (
            buf.at[sweep] for buf in (state_buf, sent_buf, back_buf, coup_buf)
        )
        state_sems, back_sems, coup_sems = (
            sems.at[sweep] for sems in (state_sem, back_sem, coup_sem)
        )
        own_state = adjoint.astype(jnp.bfloat16).astype(jnp.float32)
        state[blk] = jnp.concatenate(
            [own_state, jnp.zeros((elements, LANES - quarter), jnp.float32)], axis=1
        ).astype(jnp.bfloat16)
        for slot in range(1, slots):
            for k in range(blocks):
                send(state.at[blk], state.at[slot * blocks + blk], state_sems, away(slot, -1), k)
        to_siblings(state, state_sems)

        repeated = jnp.concatenate([own_state] * group, axis=1)
        stacked = jnp.concatenate(
            [
                jnp.where(
                    (group_col >= g * quarter) & (group_col < (g + 1) * quarter), repeated, 0.0
                )
                for g in range(group)
            ],
            axis=0,
        ).astype(jnp.bfloat16)
        lefts = jnp.dot(place_of, stacked, preferred_element_type=jnp.float32)
        turned = jnp.zeros((table, width), jnp.float32)
        for index, first in enumerate(starts):
            last = min(first + group, faces)
            depth = (last - first) * quarter
            left = lefts[index * table:(index + 1) * table, :depth].astype(jnp.bfloat16)
            turned += jnp.dot(
                left, coupling[first:last].reshape(depth, width),
                preferred_element_type=jnp.float32,
            )
        sent[:, :, :width] = turned.reshape(slots, elements, width).astype(jnp.bfloat16)
        for slot in range(1, slots):
            send(sent.at[slot], back.at[slot], back_sems, away(slot, 1), blk)

        finish(state, slots * blocks - 1, state_sems.at[1])
        every = jnp.concatenate(
            [
                jnp.concatenate(
                    [
                        state[slot * blocks + k].astype(jnp.float32)[:, :quarter]
                        for k in range(blocks)
                    ],
                    axis=1,
                )
                for slot in range(slots)
            ],
            axis=0,
        ).astype(jnp.bfloat16)
        picked = jnp.dot(pick, every, preferred_element_type=jnp.float32).astype(jnp.bfloat16)
        held = jnp.zeros((quarter, chunk * elements), jnp.float32)
        for first in range(0, faces, chunk):
            product = lax.dot_general(
                coupling[first:first + chunk].reshape(chunk * quarter, width),
                picked[first * elements:(first + chunk) * elements],
                NT,
                preferred_element_type=jnp.float32,
            )
            for f in range(chunk):
                chosen = (chunk_lane >= f * elements) & (chunk_lane < (f + 1) * elements)
                held += jnp.where(chosen, product[f * quarter:(f + 1) * quarter], 0.0)
        high = held.astype(jnp.bfloat16)
        low = (held - high.astype(jnp.float32)).astype(jnp.bfloat16)
        own_terms = lax.dot_general(
            fold, jnp.concatenate([high, low], axis=1), NT, preferred_element_type=jnp.float32
        )
        partial = turned[:elements] + in_place(own_terms)

        finish(back, slots - 1, back_sems.at[1])
        for slot in range(1, slots):
            partial += back[slot].astype(jnp.float32)[:, :width]
        coup[blk, :, :width] = partial
        to_siblings(coup, coup_sems)
        finish(coup, blocks - 1, coup_sems.at[1])
        coupled = coup[0]
        for k in range(1, blocks):
            coupled += coup[k]
        full = (coupled[:, :width] * full_mask).astype(jnp.bfloat16).astype(jnp.float32)
        return (base - invert(own_part(full), full)) * mask, full

    to_siblings(dual_buf, dual_sem)
    adjoint, full = lax.fori_loop(
        0, SWEEPS, one_sweep, (base, jnp.zeros((elements, width), jnp.float32))
    )

    result_out[:elements, :quarter] = adjoint
    finish(dual_buf, blocks - 1, dual_sem.at[1])
    dual = dual_buf[0]
    for k in range(1, blocks):
        dual += dual_buf[k]
    weights = dual[:, width:width + 1] - jnp.sum(dual[:, :width] * full, axis=1, keepdims=True)
    lane = lax.broadcasted_iota(jnp.int32, (elements, LANES), 1)
    sub = lax.broadcasted_iota(jnp.int32, (elements, LANES), 0)
    result_out[elements:elements + 1, :] = jnp.sum(
        jnp.where(lane == sub, weights, 0.0), axis=0, keepdims=True
    )

    finish(src_buf, blocks - 1, src_sem.at[0])
    finish(dual_buf, blocks - 1, dual_sem.at[0])
    for sweep in range(SWEEPS):
        finish(state_buf.at[sweep], slots * blocks - 1, state_sem.at[sweep, 0])
        finish(back_buf.at[sweep], slots - 1, back_sem.at[sweep, 0])
        finish(coup_buf.at[sweep], blocks - 1, coup_sem.at[sweep, 0])


def split_result(result, adjoint, indicator):
    elements, quarter = adjoint.shape
    adjoint[...] = result[:elements, :quarter]
    indicator[...] = result[elements:elements + 1, :elements]


def local(degree, face_elem, face_side, face_peer, coupling, inv_diag, inv_off, source, residual):
    elements, quarter = source.shape
    parts, blocks = lax.axis_size("dom"), lax.axis_size("blk")
    width = coupling.shape[2]
    slots = len(slots_of(parts)[0])
    vmem = pl.BlockSpec(memory_space=pltpu.VMEM)
    hbm = pl.BlockSpec(memory_space=pl.ANY)
    tile = (elements, LANES)
    dual_width = (width // LANES + 1) * LANES
    full_width = -(-width // LANES) * LANES
    dma = pltpu.SemaphoreType.DMA
    args = (degree, face_elem, face_side, face_peer, coupling, inv_diag, inv_off, source, residual)
    result = pl.pallas_call(
        functools.partial(kernel, parts, blocks),
        out_shape=jax.ShapeDtypeStruct((2 * elements, LANES), jnp.float32),
        in_specs=[hbm] * len(args),
        out_specs=vmem,
        scratch_shapes=[pltpu.SMEM(arg.shape, arg.dtype) for arg in args[:4]]
        + [pltpu.VMEM(arg.shape, arg.dtype) for arg in args[4:]]
        + [
            pltpu.VMEM((blocks,) + tile, jnp.float32),
            pltpu.VMEM((SWEEPS, slots * blocks) + tile, jnp.bfloat16),
            pltpu.VMEM((SWEEPS, slots, elements, full_width), jnp.bfloat16),
            pltpu.VMEM((SWEEPS, slots, elements, full_width), jnp.bfloat16),
            pltpu.VMEM((SWEEPS, blocks, elements, full_width), jnp.float32),
            pltpu.VMEM((blocks, elements, dual_width), jnp.float32),
            dma((len(args),)), dma((2,)), dma((2,)),
        ]
        + [dma((SWEEPS, 2))] * 3,
        compiler_params=pltpu.CompilerParams(
            collective_id=0, has_side_effects=True, vmem_limit_bytes=60 * 2**20
        ),
    )(*args)
    adjoint, indicator = pl.pallas_call(
        split_result,
        out_shape=(
            jax.ShapeDtypeStruct((elements, quarter), jnp.float32),
            jax.ShapeDtypeStruct((1, elements), jnp.float32),
        ),
        in_specs=[vmem],
        out_specs=(vmem, vmem),
        compiler_params=pltpu.CompilerParams(vmem_limit_bytes=60 * 2**20),
    )(result)
    return adjoint, indicator.reshape(elements)


def solution(mesh):
    in_specs = (
        P("dom"),
        P("dom"),
        P("dom"),
        P("dom"),
        P("dom", "blk", None),
        P("dom", "blk"),
        P("dom", "blk", None),
        P("dom", "blk"),
        P("dom", "blk"),
    )
    out_specs = (P("dom", "blk"), P("dom"))
    return jax.shard_map(local, mesh=mesh, in_specs=in_specs, out_specs=out_specs, check_vma=False)
```

```python
import functools
import math

import jax
import jax.numpy as jnp
from jax import lax
from jax.experimental import pallas as pl
from jax.experimental.pallas import tpu as pltpu
from jax.sharding import PartitionSpec as P

MODES = 64
SWEEPS = 2
NEIGH = 8
LANES = 128
MESH = pl.DeviceIdType.MESH
NT = (((1,), (1,)), ((), ()))


def slots_of(parts):
    half = NEIGH // 2
    offsets = [0] + list(range(1, half + 1)) + [-k for k in range(1, half + 1)]
    unique, side_slot = [], []
    for offset in offsets:
        wrapped = offset % parts
        if wrapped not in unique:
            unique.append(wrapped)
        side_slot.append(unique.index(wrapped))
    return unique, side_slot


def kernel(
    parts, blocks,
    degree_hbm, elem_hbm, side_hbm, peer_hbm, coupling_hbm, diag_hbm, inv_off_hbm, source_hbm,
    residual_hbm,
    result_out,
    degree, face_elem, face_side, face_peer, coupling, inv_diag, inv_off, source, residual,
    src_buf, state_buf, sent_buf, back_buf, coup_buf, dual_buf,
    load_sem, src_sem, dual_sem, state_sem, back_sem, coup_sem,
):
    unique, side_slot = slots_of(parts)
    slots = len(unique)
    elements, quarter = source.shape
    faces, _, width = coupling.shape
    table = slots * elements
    dom = lax.axis_index("dom")
    blk = lax.axis_index("blk")

    siblings = [lax.rem(blk + step, blocks) for step in range(1, blocks)]

    def away(slot, sign):
        return lax.rem(dom + (sign * unique[slot]) % parts, parts)

    barrier = pltpu.get_barrier_semaphore()
    for slot in range(1, slots):
        for k in range(blocks):
            pl.semaphore_signal(
                barrier, inc=1, device_id=(away(slot, 1), k), device_id_type=MESH
            )
    for k in siblings:
        pl.semaphore_signal(barrier, inc=1, device_id=(dom, k), device_id_type=MESH)

    loads = [
        pltpu.make_async_copy(src, dst, load_sem.at[place])
        for place, (src, dst) in enumerate([
            (degree_hbm, degree), (source_hbm, source), (elem_hbm, face_elem),
            (side_hbm, face_side), (peer_hbm, face_peer), (diag_hbm, inv_diag),
            (residual_hbm, residual), (inv_off_hbm, inv_off), (coupling_hbm, coupling),
        ])
    ]
    for load in loads:
        load.start()

    def send(src, dst, sems, there, k):
        pltpu.make_async_remote_copy(
            src_ref=src, dst_ref=dst, send_sem=sems.at[0], recv_sem=sems.at[1],
            device_id=(there, k), device_id_type=MESH,
        ).start()

    def finish(buf, count, sem):
        part = buf.at[pl.ds(0, count)]
        pltpu.make_async_copy(part, part, sem).wait()

    def to_siblings(buf, sems):
        for k in siblings:
            send(buf.at[blk], buf.at[blk], sems, dom, k)

    def joined(buf, rows):
        return jnp.concatenate(
            [buf[k][:rows, :quarter].astype(jnp.float32) for k in range(blocks)], axis=1
        )

    row = lax.broadcasted_iota(jnp.int32, (elements, quarter), 0)
    mode = (lax.broadcasted_iota(jnp.int32, (elements, quarter), 1) + blk * quarter) % MODES
    full_row = lax.broadcasted_iota(jnp.int32, (elements, width), 0)
    full_col = lax.broadcasted_iota(jnp.int32, (elements, width), 1)
    mine = (full_col >= blk * quarter) & (full_col < (blk + 1) * quarter)

    def in_place(values):
        return jnp.where(mine, jnp.concatenate([values] * blocks, axis=1), 0.0)

    def own_part(values):
        found = values[:, :quarter]
        for k in range(1, blocks):
            found = jnp.where(blk == k, values[:, k * quarter:(k + 1) * quarter], found)
        return found

    limit = jnp.zeros((elements, quarter), jnp.int32)
    full_limit = jnp.zeros((elements, width), jnp.int32)
    loads[0].wait()
    for e in range(elements):
        step = degree[e] + 1
        count = step * step * step * MODES // 64
        limit = jnp.where(row == e, count, limit)
        full_limit = jnp.where(full_row == e, count, full_limit)
    mask = (mode < limit).astype(jnp.float32)
    full_mask = (full_col % MODES < full_limit).astype(jnp.float32)
    loads[1].wait()
    src_half = (source[...] * mask).astype(jnp.bfloat16).astype(jnp.float32)
    src_buf[blk, :, :quarter] = src_half

    for load in loads[2:7]:
        load.wait()
    owner = [face_elem[f] for f in range(faces)]
    target = []
    for f in range(faces):
        side = face_side[f]
        slot = side
        for s, wanted in enumerate(side_slot):
            if wanted != s:
                slot = jnp.where(side == s, wanted, slot)
        target.append(slot * elements + face_peer[f])

    pick_row = lax.broadcasted_iota(jnp.int32, (elements, table), 0)
    pick_col = lax.broadcasted_iota(jnp.int32, (elements, table), 1)
    pick = jnp.concatenate(
        [
            jnp.where((pick_row == owner[f]) & (pick_col == target[f]), 1.0, 0.0)
            for f in range(faces)
        ],
        axis=0,
    ).astype(jnp.bfloat16)
    group = max(1, 256 // quarter)
    starts = list(range(0, faces, group))
    spread_row = lax.broadcasted_iota(jnp.int32, (table, group * elements), 0)
    spread_col = lax.broadcasted_iota(jnp.int32, (table, group * elements), 1)
    place_of = []
    for first in starts:
        hot = jnp.zeros((table, group * elements), jnp.float32)
        for f in range(first, min(first + group, faces)):
            col = (f - first) * elements + owner[f]
            hot = jnp.where((spread_row == target[f]) & (spread_col == col), 1.0, hot)
        place_of.append(hot)
    place_of = jnp.concatenate(place_of, axis=0).astype(jnp.bfloat16)
    group_col = lax.broadcasted_iota(jnp.int32, (elements, group * quarter), 1)
    chunk = math.gcd(faces, max(1, LANES // elements))
    chunk_lane = lax.broadcasted_iota(jnp.int32, (quarter, chunk * elements), 1)
    fold_row = lax.broadcasted_iota(jnp.int32, (elements, 2 * chunk * elements), 0)
    fold_col = lax.broadcasted_iota(jnp.int32, (elements, 2 * chunk * elements), 1)
    fold = jnp.where(fold_col % elements == fold_row, 1.0, 0.0).astype(jnp.bfloat16)

    pl.semaphore_wait(barrier, slots * blocks - 1)
    to_siblings(src_buf, src_sem)

    weight = residual[...] * mask
    high = weight.astype(jnp.bfloat16).astype(jnp.float32)
    low = weight - high
    row16 = lax.broadcasted_iota(jnp.int32, (2 * elements, quarter), 0)
    both = jnp.concatenate([high, low], axis=0)
    loads[7].wait()
    dual = jnp.zeros((2 * elements, width), jnp.float32)
    for e in range(elements):
        left = jnp.where((row16 == e) | (row16 == e + elements), both, 0.0).astype(jnp.bfloat16)
        dual += jnp.dot(left, inv_off[e], preferred_element_type=jnp.float32)
    dual = dual[:elements] + dual[elements:]
    dual_buf[blk, :, :width] = dual + in_place(weight * inv_diag[...])

    def invert(own, full):
        total = inv_diag[...] * own
        for e in range(elements):
            left = jnp.where(full_row == e, full, 0.0).astype(jnp.bfloat16)
            total += lax.dot_general(left, inv_off[e], NT, preferred_element_type=jnp.float32)
        return total

    finish(src_buf, blocks - 1, src_sem.at[1])
    base = invert(src_half, joined(src_buf, elements)) * mask
    dual_buf[blk, :, width:] = jnp.broadcast_to(
        jnp.sum(weight * base, axis=1, keepdims=True), (elements, dual_buf.shape[2] - width)
    )
    loads[8].wait()

    to_siblings(dual_buf, dual_sem)
    adjoint = base
    for sweep in range(SWEEPS):
        state, sent, back, coup = (
            buf.at[sweep] for buf in (state_buf, sent_buf, back_buf, coup_buf)
        )
        state_sems, back_sems, coup_sems = (
            sems.at[sweep] for sems in (state_sem, back_sem, coup_sem)
        )
        own_state = adjoint.astype(jnp.bfloat16).astype(jnp.float32)
        state[blk] = jnp.concatenate(
            [own_state, jnp.zeros((elements, LANES - quarter), jnp.float32)], axis=1
        ).astype(jnp.bfloat16)
        pending = [(slot, away(slot, -1), k) for slot in range(1, slots) for k in range(blocks)]
        pending += [(0, dom, k) for k in siblings]
        each = -(-len(pending) // (len(starts) + 1))

        def send_some():
            for slot, there, k in pending[:each]:
                send(state.at[blk], state.at[slot * blocks + blk], state_sems, there, k)
            del pending[:each]

        send_some()

        repeated = jnp.concatenate([own_state] * group, axis=1)
        stacked = jnp.concatenate(
            [
                jnp.where(
                    (group_col >= g * quarter) & (group_col < (g + 1) * quarter), repeated, 0.0
                )
                for g in range(group)
            ],
            axis=0,
        ).astype(jnp.bfloat16)
        lefts = jnp.dot(place_of, stacked, preferred_element_type=jnp.float32)
        turned = jnp.zeros((table, width), jnp.float32)
        for index, first in enumerate(starts):
            last = min(first + group, faces)
            depth = (last - first) * quarter
            left = lefts[index * table:(index + 1) * table, :depth].astype(jnp.bfloat16)
            turned += jnp.dot(
                left, coupling[first:last].reshape(depth, width),
                preferred_element_type=jnp.float32,
            )
            send_some()
        sent[:, :, :width] = turned.reshape(slots, elements, width).astype(jnp.bfloat16)
        for slot in range(1, slots):
            send(sent.at[slot], back.at[slot], back_sems, away(slot, 1), blk)

        finish(state, slots * blocks - 1, state_sems.at[1])
        every = jnp.concatenate(
            [
                jnp.concatenate(
                    [
                        state[slot * blocks + k].astype(jnp.float32)[:, :quarter]
                        for k in range(blocks)
                    ],
                    axis=1,
                )
                for slot in range(slots)
            ],
            axis=0,
        ).astype(jnp.bfloat16)
        picked = jnp.dot(pick, every, preferred_element_type=jnp.float32).astype(jnp.bfloat16)
        held = jnp.zeros((quarter, chunk * elements), jnp.float32)
        for first in range(0, faces, chunk):
            product = lax.dot_general(
                coupling[first:first + chunk].reshape(chunk * quarter, width),
                picked[first * elements:(first + chunk) * elements],
                NT,
                preferred_element_type=jnp.float32,
            )
            for f in range(chunk):
                chosen = (chunk_lane >= f * elements) & (chunk_lane < (f + 1) * elements)
                held += jnp.where(chosen, product[f * quarter:(f + 1) * quarter], 0.0)
        high = held.astype(jnp.bfloat16)
        low = (held - high.astype(jnp.float32)).astype(jnp.bfloat16)
        own_terms = lax.dot_general(
            fold, jnp.concatenate([high, low], axis=1), NT, preferred_element_type=jnp.float32
        )
        partial = turned[:elements] + in_place(own_terms)

        finish(back, slots - 1, back_sems.at[1])
        for slot in range(1, slots):
            partial += back[slot].astype(jnp.float32)[:, :width]
        coup[blk, :, :width] = partial
        to_siblings(coup, coup_sems)
        if sweep == SWEEPS - 1:
            finish(dual_buf, blocks - 1, dual_sem.at[1])
            dual = dual_buf[0]
            for k in range(1, blocks):
                dual += dual_buf[k]
        finish(coup, blocks - 1, coup_sems.at[1])
        coupled = coup[0]
        for k in range(1, blocks):
            coupled += coup[k]
        full = (coupled[:, :width] * full_mask).astype(jnp.bfloat16).astype(jnp.float32)
        adjoint = (base - invert(own_part(full), full)) * mask

    result_out[:elements, :quarter] = adjoint
    weights = dual[:, width:width + 1] - jnp.sum(dual[:, :width] * full, axis=1, keepdims=True)
    lane = lax.broadcasted_iota(jnp.int32, (elements, LANES), 1)
    sub = lax.broadcasted_iota(jnp.int32, (elements, LANES), 0)
    result_out[elements:elements + 1, :] = jnp.sum(
        jnp.where(lane == sub, weights, 0.0), axis=0, keepdims=True
    )

    finish(src_buf, blocks - 1, src_sem.at[0])
    finish(dual_buf, blocks - 1, dual_sem.at[0])
    for sweep in range(SWEEPS):
        finish(state_buf.at[sweep], slots * blocks - 1, state_sem.at[sweep, 0])
        finish(back_buf.at[sweep], slots - 1, back_sem.at[sweep, 0])
        finish(coup_buf.at[sweep], blocks - 1, coup_sem.at[sweep, 0])


def split_result(result, adjoint, indicator):
    elements, quarter = adjoint.shape
    adjoint[...] = result[:elements, :quarter]
    indicator[...] = result[elements:elements + 1, :elements]


def local(degree, face_elem, face_side, face_peer, coupling, inv_diag, inv_off, source, residual):
    elements, quarter = source.shape
    parts, blocks = lax.axis_size("dom"), lax.axis_size("blk")
    width = coupling.shape[2]
    slots = len(slots_of(parts)[0])
    vmem = pl.BlockSpec(memory_space=pltpu.VMEM)
    hbm = pl.BlockSpec(memory_space=pl.ANY)
    tile = (elements, LANES)
    dual_width = (width // LANES + 1) * LANES
    full_width = -(-width // LANES) * LANES
    dma = pltpu.SemaphoreType.DMA
    args = (degree, face_elem, face_side, face_peer, coupling, inv_diag, inv_off, source, residual)
    result = pl.pallas_call(
        functools.partial(kernel, parts, blocks),
        out_shape=jax.ShapeDtypeStruct((2 * elements, LANES), jnp.float32),
        in_specs=[hbm] * len(args),
        out_specs=vmem,
        scratch_shapes=[pltpu.SMEM(arg.shape, arg.dtype) for arg in args[:4]]
        + [pltpu.VMEM(arg.shape, arg.dtype) for arg in args[4:]]
        + [
            pltpu.VMEM((blocks,) + tile, jnp.float32),
            pltpu.VMEM((SWEEPS, slots * blocks) + tile, jnp.bfloat16),
            pltpu.VMEM((SWEEPS, slots, elements, full_width), jnp.bfloat16),
            pltpu.VMEM((SWEEPS, slots, elements, full_width), jnp.bfloat16),
            pltpu.VMEM((SWEEPS, blocks, elements, full_width), jnp.float32),
            pltpu.VMEM((blocks, elements, dual_width), jnp.float32),
            dma((len(args),)), dma((2,)), dma((2,)),
        ]
        + [dma((SWEEPS, 2))] * 3,
        compiler_params=pltpu.CompilerParams(
            collective_id=0, has_side_effects=True, vmem_limit_bytes=60 * 2**20
        ),
    )(*args)
    adjoint, indicator = pl.pallas_call(
        split_result,
        out_shape=(
            jax.ShapeDtypeStruct((elements, quarter), jnp.float32),
            jax.ShapeDtypeStruct((1, elements), jnp.float32),
        ),
        in_specs=[vmem],
        out_specs=(vmem, vmem),
        compiler_params=pltpu.CompilerParams(vmem_limit_bytes=60 * 2**20),
    )(result)
    return adjoint, indicator.reshape(elements)


def solution(mesh):
    in_specs = (
        P("dom"),
        P("dom"),
        P("dom"),
        P("dom"),
        P("dom", "blk", None),
        P("dom", "blk"),
        P("dom", "blk", None),
        P("dom", "blk"),
        P("dom", "blk"),
    )
    out_specs = (P("dom", "blk"), P("dom"))
    return jax.shard_map(local, mesh=mesh, in_specs=in_specs, out_specs=out_specs, check_vma=False)
```

```python
import functools
import math

import jax
import jax.numpy as jnp
from jax import lax
from jax.experimental import pallas as pl
from jax.experimental.pallas import tpu as pltpu
from jax.sharding import PartitionSpec as P

MODES = 64
SWEEPS = 2
NEIGH = 8
LANES = 128
MESH = pl.DeviceIdType.MESH
NT = (((1,), (1,)), ((), ()))


def slots_of(parts):
    half = NEIGH // 2
    offsets = [0] + list(range(1, half + 1)) + [-k for k in range(1, half + 1)]
    unique, side_slot = [], []
    for offset in offsets:
        wrapped = offset % parts
        if wrapped not in unique:
            unique.append(wrapped)
        side_slot.append(unique.index(wrapped))
    return unique, side_slot


def kernel(
    parts, blocks,
    degree_hbm, elem_hbm, side_hbm, peer_hbm, coupling_hbm, diag_hbm, inv_off_hbm, source_hbm,
    residual_hbm,
    result_out,
    degree, face_elem, face_side, face_peer, coupling, inv_diag, inv_off, source, residual,
    src_buf, state_buf, sent_buf, back_buf, coup_buf, dual_buf,
    load_sem, src_sem, dual_sem, state_sem, back_sem, coup_sem,
):
    unique, side_slot = slots_of(parts)
    slots = len(unique)
    elements, quarter = source.shape
    faces, _, width = coupling.shape
    table = slots * elements
    dom = lax.axis_index("dom")
    blk = lax.axis_index("blk")

    siblings = [lax.rem(blk + step, blocks) for step in range(1, blocks)]

    def away(slot, sign):
        return lax.rem(dom + (sign * unique[slot]) % parts, parts)

    far_first = sorted(range(1, slots), key=lambda slot: -min(unique[slot], parts - unique[slot]))
    barrier = pltpu.get_barrier_semaphore()
    for slot in far_first:
        for k in range(blocks):
            pl.semaphore_signal(
                barrier, inc=1, device_id=(away(slot, 1), k), device_id_type=MESH
            )
    for k in siblings:
        pl.semaphore_signal(barrier, inc=1, device_id=(dom, k), device_id_type=MESH)

    loads = [
        pltpu.make_async_copy(src, dst, load_sem.at[place])
        for place, (src, dst) in enumerate([
            (degree_hbm, degree), (source_hbm, source), (elem_hbm, face_elem),
            (side_hbm, face_side), (peer_hbm, face_peer), (diag_hbm, inv_diag),
            (residual_hbm, residual), (inv_off_hbm, inv_off), (coupling_hbm, coupling),
        ])
    ]
    for load in loads:
        load.start()

    def send(src, dst, sems, there, k):
        pltpu.make_async_remote_copy(
            src_ref=src, dst_ref=dst, send_sem=sems.at[0], recv_sem=sems.at[1],
            device_id=(there, k), device_id_type=MESH,
        ).start()

    def finish(buf, count, sem):
        part = buf.at[pl.ds(0, count)]
        pltpu.make_async_copy(part, part, sem).wait()

    def to_siblings(buf, sems):
        for k in siblings:
            send(buf.at[blk], buf.at[blk], sems, dom, k)

    def joined(buf, rows):
        return jnp.concatenate(
            [buf[k][:rows, :quarter].astype(jnp.float32) for k in range(blocks)], axis=1
        )

    row = lax.broadcasted_iota(jnp.int32, (elements, quarter), 0)
    mode = (lax.broadcasted_iota(jnp.int32, (elements, quarter), 1) + blk * quarter) % MODES
    full_row = lax.broadcasted_iota(jnp.int32, (elements, width), 0)
    full_col = lax.broadcasted_iota(jnp.int32, (elements, width), 1)
    mine = (full_col >= blk * quarter) & (full_col < (blk + 1) * quarter)

    def in_place(values):
        return jnp.where(mine, jnp.concatenate([values] * blocks, axis=1), 0.0)

    def own_part(values):
        found = values[:, :quarter]
        for k in range(1, blocks):
            found = jnp.where(blk == k, values[:, k * quarter:(k + 1) * quarter], found)
        return found

    limit = jnp.zeros((elements, quarter), jnp.int32)
    full_limit = jnp.zeros((elements, width), jnp.int32)
    loads[0].wait()
    for e in range(elements):
        step = degree[e] + 1
        count = step * step * step * MODES // 64
        limit = jnp.where(row == e, count, limit)
        full_limit = jnp.where(full_row == e, count, full_limit)
    mask = (mode < limit).astype(jnp.float32)
    full_mask = (full_col % MODES < full_limit).astype(jnp.float32)
    loads[1].wait()
    src_half = (source[...] * mask).astype(jnp.bfloat16).astype(jnp.float32)
    src_buf[blk, :, :quarter] = src_half

    for load in loads[2:7]:
        load.wait()
    owner = [face_elem[f] for f in range(faces)]
    target = []
    for f in range(faces):
        side = face_side[f]
        slot = side
        for s, wanted in enumerate(side_slot):
            if wanted != s:
                slot = jnp.where(side == s, wanted, slot)
        target.append(slot * elements + face_peer[f])

    pick_row = lax.broadcasted_iota(jnp.int32, (elements, table), 0)
    pick_col = lax.broadcasted_iota(jnp.int32, (elements, table), 1)
    pick = jnp.concatenate(
        [
            jnp.where((pick_row == owner[f]) & (pick_col == target[f]), 1.0, 0.0)
            for f in range(faces)
        ],
        axis=0,
    ).astype(jnp.bfloat16)
    group = max(1, 256 // quarter)
    starts = list(range(0, faces, group))
    spread_row = lax.broadcasted_iota(jnp.int32, (table, group * elements), 0)
    spread_col = lax.broadcasted_iota(jnp.int32, (table, group * elements), 1)
    place_of = []
    for first in starts:
        hot = jnp.zeros((table, group * elements), jnp.float32)
        for f in range(first, min(first + group, faces)):
            col = (f - first) * elements + owner[f]
            hot = jnp.where((spread_row == target[f]) & (spread_col == col), 1.0, hot)
        place_of.append(hot)
    place_of = jnp.concatenate(place_of, axis=0).astype(jnp.bfloat16)
    group_col = lax.broadcasted_iota(jnp.int32, (elements, group * quarter), 1)
    table_lane = lax.broadcasted_iota(jnp.int32, (table, LANES), 1)
    chunk = math.gcd(faces, max(1, LANES // elements))
    chunk_lane = lax.broadcasted_iota(jnp.int32, (quarter, chunk * elements), 1)
    fold_row = lax.broadcasted_iota(jnp.int32, (elements, 2 * chunk * elements), 0)
    fold_col = lax.broadcasted_iota(jnp.int32, (elements, 2 * chunk * elements), 1)
    fold = jnp.where(fold_col % elements == fold_row, 1.0, 0.0).astype(jnp.bfloat16)

    pl.semaphore_wait(barrier, slots * blocks - 1)
    to_siblings(src_buf, src_sem)

    weight = residual[...] * mask
    high = weight.astype(jnp.bfloat16).astype(jnp.float32)
    low = weight - high
    row16 = lax.broadcasted_iota(jnp.int32, (2 * elements, quarter), 0)
    both = jnp.concatenate([high, low], axis=0)
    loads[7].wait()
    dual = jnp.zeros((2 * elements, width), jnp.float32)
    for e in range(elements):
        left = jnp.where((row16 == e) | (row16 == e + elements), both, 0.0).astype(jnp.bfloat16)
        dual += jnp.dot(left, inv_off[e], preferred_element_type=jnp.float32)
    dual = dual[:elements] + dual[elements:]
    dual_buf[blk, :, :width] = dual + in_place(weight * inv_diag[...])

    def invert(own, full):
        total = inv_diag[...] * own
        for e in range(elements):
            left = jnp.where(full_row == e, full, 0.0).astype(jnp.bfloat16)
            total += lax.dot_general(left, inv_off[e], NT, preferred_element_type=jnp.float32)
        return total

    finish(src_buf, blocks - 1, src_sem.at[1])
    base = invert(src_half, joined(src_buf, elements)) * mask
    dual_buf[blk, :, width:] = jnp.broadcast_to(
        jnp.sum(weight * base, axis=1, keepdims=True), (elements, dual_buf.shape[2] - width)
    )
    loads[8].wait()

    def one_sweep(sweep, carry):
        adjoint, _ = carry
        state, sent, back, coup = (
            buf.at[sweep] for buf in (state_buf, sent_buf, back_buf, coup_buf)
        )
        state_sems, back_sems, coup_sems = (
            sems.at[sweep] for sems in (state_sem, back_sem, coup_sem)
        )
        own_state = adjoint.astype(jnp.bfloat16).astype(jnp.float32)
        block = jnp.concatenate(
            [own_state, jnp.zeros((elements, LANES - quarter), jnp.float32)], axis=1
        )
        turned_block = block
        for k in range(1, blocks):
            turned_block = jnp.where(
                blk == k, pltpu.roll(block, k * quarter % LANES, 1), turned_block
            )
        state[blk] = turned_block.astype(jnp.bfloat16)
        for slot in far_first:
            for k in range(blocks):
                send(state.at[blk], state.at[slot * blocks + blk], state_sems, away(slot, -1), k)
        to_siblings(state, state_sems)

        repeated = jnp.concatenate([own_state] * group, axis=1)
        stacked = jnp.concatenate(
            [
                jnp.where(
                    (group_col >= g * quarter) & (group_col < (g + 1) * quarter), repeated, 0.0
                )
                for g in range(group)
            ],
            axis=0,
        ).astype(jnp.bfloat16)
        lefts = jnp.dot(place_of, stacked, preferred_element_type=jnp.float32)
        turned = jnp.zeros((table, width), jnp.float32)
        for index, first in enumerate(starts):
            last = min(first + group, faces)
            depth = (last - first) * quarter
            left = lefts[index * table:(index + 1) * table, :depth].astype(jnp.bfloat16)
            turned += jnp.dot(
                left, coupling[first:last].reshape(depth, width),
                preferred_element_type=jnp.float32,
            )
        sent[:, :, :width] = turned.reshape(slots, elements, width).astype(jnp.bfloat16)
        for slot in far_first:
            send(sent.at[slot], back.at[slot], back_sems, away(slot, 1), blk)

        finish(state, slots * blocks - 1, state_sems.at[1])
        columns = [
            jnp.concatenate(
                [state[slot * blocks + k].astype(jnp.float32) for slot in range(slots)], axis=0
            )
            for k in range(blocks)
        ]
        tiles = []
        for start in range(0, width, LANES):
            inside = [k for k in range(blocks)
                      if k * quarter < start + LANES and (k + 1) * quarter > start]
            joint = columns[inside[-1]]
            for k in inside[-2::-1]:
                joint = jnp.where(table_lane < (k + 1) * quarter - start, columns[k], joint)
            tiles.append(joint)
        every = jnp.concatenate(tiles, axis=1)[:, :width].astype(jnp.bfloat16)
        picked = jnp.dot(pick, every, preferred_element_type=jnp.float32).astype(jnp.bfloat16)
        held = jnp.zeros((quarter, chunk * elements), jnp.float32)
        for first in range(0, faces, chunk):
            product = lax.dot_general(
                coupling[first:first + chunk].reshape(chunk * quarter, width),
                picked[first * elements:(first + chunk) * elements],
                NT,
                preferred_element_type=jnp.float32,
            )
            for f in range(chunk):
                chosen = (chunk_lane >= f * elements) & (chunk_lane < (f + 1) * elements)
                held += jnp.where(chosen, product[f * quarter:(f + 1) * quarter], 0.0)
        high = held.astype(jnp.bfloat16)
        low = (held - high.astype(jnp.float32)).astype(jnp.bfloat16)
        own_terms = lax.dot_general(
            fold, jnp.concatenate([high, low], axis=1), NT, preferred_element_type=jnp.float32
        )
        partial = turned[:elements] + in_place(own_terms)

        finish(back, slots - 1, back_sems.at[1])
        for slot in range(1, slots):
            partial += back[slot].astype(jnp.float32)[:, :width]
        coup[blk, :, :width] = partial
        to_siblings(coup, coup_sems)
        finish(coup, blocks - 1, coup_sems.at[1])
        coupled = coup[0]
        for k in range(1, blocks):
            coupled += coup[k]
        full = (coupled[:, :width] * full_mask).astype(jnp.bfloat16).astype(jnp.float32)
        return (base - invert(own_part(full), full)) * mask, full

    to_siblings(dual_buf, dual_sem)
    adjoint, full = lax.fori_loop(
        0, SWEEPS, one_sweep, (base, jnp.zeros((elements, width), jnp.float32))
    )

    result_out[:elements, :quarter] = adjoint
    finish(dual_buf, blocks - 1, dual_sem.at[1])
    dual = dual_buf[0]
    for k in range(1, blocks):
        dual += dual_buf[k]
    weights = dual[:, width:width + 1] - jnp.sum(dual[:, :width] * full, axis=1, keepdims=True)
    lane = lax.broadcasted_iota(jnp.int32, (elements, LANES), 1)
    sub = lax.broadcasted_iota(jnp.int32, (elements, LANES), 0)
    result_out[elements:elements + 1, :] = jnp.sum(
        jnp.where(lane == sub, weights, 0.0), axis=0, keepdims=True
    )

    finish(src_buf, blocks - 1, src_sem.at[0])
    finish(dual_buf, blocks - 1, dual_sem.at[0])
    for sweep in range(SWEEPS):
        finish(state_buf.at[sweep], slots * blocks - 1, state_sem.at[sweep, 0])
        finish(back_buf.at[sweep], slots - 1, back_sem.at[sweep, 0])
        finish(coup_buf.at[sweep], blocks - 1, coup_sem.at[sweep, 0])


def split_result(result, adjoint, indicator):
    elements, quarter = adjoint.shape
    adjoint[...] = result[:elements, :quarter]
    indicator[...] = result[elements:elements + 1, :elements]


def local(degree, face_elem, face_side, face_peer, coupling, inv_diag, inv_off, source, residual):
    elements, quarter = source.shape
    parts, blocks = lax.axis_size("dom"), lax.axis_size("blk")
    width = coupling.shape[2]
    slots = len(slots_of(parts)[0])
    vmem = pl.BlockSpec(memory_space=pltpu.VMEM)
    hbm = pl.BlockSpec(memory_space=pl.ANY)
    tile = (elements, LANES)
    dual_width = (width // LANES + 1) * LANES
    full_width = -(-width // LANES) * LANES
    dma = pltpu.SemaphoreType.DMA
    args = (degree, face_elem, face_side, face_peer, coupling, inv_diag, inv_off, source, residual)
    result = pl.pallas_call(
        functools.partial(kernel, parts, blocks),
        out_shape=jax.ShapeDtypeStruct((2 * elements, LANES), jnp.float32),
        in_specs=[hbm] * len(args),
        out_specs=vmem,
        scratch_shapes=[pltpu.SMEM(arg.shape, arg.dtype) for arg in args[:4]]
        + [pltpu.VMEM(arg.shape, arg.dtype) for arg in args[4:]]
        + [
            pltpu.VMEM((blocks,) + tile, jnp.float32),
            pltpu.VMEM((SWEEPS, slots * blocks) + tile, jnp.bfloat16),
            pltpu.VMEM((SWEEPS, slots, elements, full_width), jnp.bfloat16),
            pltpu.VMEM((SWEEPS, slots, elements, full_width), jnp.bfloat16),
            pltpu.VMEM((SWEEPS, blocks, elements, full_width), jnp.float32),
            pltpu.VMEM((blocks, elements, dual_width), jnp.float32),
            dma((len(args),)), dma((2,)), dma((2,)),
        ]
        + [dma((SWEEPS, 2))] * 3,
        compiler_params=pltpu.CompilerParams(
            collective_id=0, has_side_effects=True, vmem_limit_bytes=60 * 2**20
        ),
    )(*args)
    adjoint, indicator = pl.pallas_call(
        split_result,
        out_shape=(
            jax.ShapeDtypeStruct((elements, quarter), jnp.float32),
            jax.ShapeDtypeStruct((1, elements), jnp.float32),
        ),
        in_specs=[vmem],
        out_specs=(vmem, vmem),
        compiler_params=pltpu.CompilerParams(vmem_limit_bytes=60 * 2**20),
    )(result)
    return adjoint, indicator.reshape(elements)


def solution(mesh):
    in_specs = (
        P("dom"),
        P("dom"),
        P("dom"),
        P("dom"),
        P("dom", "blk", None),
        P("dom", "blk"),
        P("dom", "blk", None),
        P("dom", "blk"),
        P("dom", "blk"),
    )
    out_specs = (P("dom", "blk"), P("dom"))
    return jax.shard_map(local, mesh=mesh, in_specs=in_specs, out_specs=out_specs, check_vma=False)
```

```python
import functools
import math

import jax
import jax.numpy as jnp
from jax import lax
from jax.experimental import pallas as pl
from jax.experimental.pallas import tpu as pltpu
from jax.sharding import PartitionSpec as P

MODES = 64
SWEEPS = 2
NEIGH = 8
LANES = 128
MESH = pl.DeviceIdType.MESH
NT = (((1,), (1,)), ((), ()))


def slots_of(parts):
    half = NEIGH // 2
    offsets = [0] + list(range(1, half + 1)) + [-k for k in range(1, half + 1)]
    unique, side_slot = [], []
    for offset in offsets:
        wrapped = offset % parts
        if wrapped not in unique:
            unique.append(wrapped)
        side_slot.append(unique.index(wrapped))
    return unique, side_slot


def kernel(
    parts, blocks,
    degree_hbm, elem_hbm, side_hbm, peer_hbm, coupling_hbm, diag_hbm, inv_off_hbm, source_hbm,
    residual_hbm,
    result_out,
    degree, face_elem, face_side, face_peer, coupling, inv_diag, inv_off, source, residual,
    src_buf, state_buf, sent_buf, back_buf, coup_buf, dual_buf,
    load_sem, src_sem, dual_sem, state_sem, back_sem, coup_sem,
):
    unique, side_slot = slots_of(parts)
    slots = len(unique)
    elements, quarter = source.shape
    faces, _, width = coupling.shape
    table = slots * elements
    dom = lax.axis_index("dom")
    blk = lax.axis_index("blk")

    loads = [
        pltpu.make_async_copy(src, dst, load_sem.at[place])
        for place, (src, dst) in enumerate([
            (degree_hbm, degree), (source_hbm, source), (elem_hbm, face_elem),
            (side_hbm, face_side), (peer_hbm, face_peer), (diag_hbm, inv_diag),
            (residual_hbm, residual), (inv_off_hbm, inv_off), (coupling_hbm, coupling),
        ])
    ]
    for load in loads:
        load.start()

    siblings = [lax.rem(blk + step, blocks) for step in range(1, blocks)]

    def away(slot, sign):
        return lax.rem(dom + (sign * unique[slot]) % parts, parts)

    far_first = sorted(range(1, slots), key=lambda slot: -min(unique[slot], parts - unique[slot]))
    barrier = pltpu.get_barrier_semaphore()
    for slot in far_first:
        for k in range(blocks):
            pl.semaphore_signal(
                barrier, inc=1, device_id=(away(slot, 1), k), device_id_type=MESH
            )
    for k in siblings:
        pl.semaphore_signal(barrier, inc=1, device_id=(dom, k), device_id_type=MESH)

    def send(src, dst, sems, there, k):
        pltpu.make_async_remote_copy(
            src_ref=src, dst_ref=dst, send_sem=sems.at[0], recv_sem=sems.at[1],
            device_id=(there, k), device_id_type=MESH,
        ).start()

    def finish(buf, count, sem):
        part = buf.at[pl.ds(0, count)]
        pltpu.make_async_copy(part, part, sem).wait()

    def to_siblings(buf, sems):
        for k in siblings:
            send(buf.at[blk], buf.at[blk], sems, dom, k)

    def joined(buf, rows):
        return jnp.concatenate(
            [buf[k][:rows, :quarter].astype(jnp.float32) for k in range(blocks)], axis=1
        )

    row = lax.broadcasted_iota(jnp.int32, (elements, quarter), 0)
    mode = (lax.broadcasted_iota(jnp.int32, (elements, quarter), 1) + blk * quarter) % MODES
    full_row = lax.broadcasted_iota(jnp.int32, (elements, width), 0)
    full_col = lax.broadcasted_iota(jnp.int32, (elements, width), 1)
    mine = (full_col >= blk * quarter) & (full_col < (blk + 1) * quarter)

    def in_place(values):
        return jnp.where(mine, jnp.concatenate([values] * blocks, axis=1), 0.0)

    def own_part(values):
        found = values[:, :quarter]
        for k in range(1, blocks):
            found = jnp.where(blk == k, values[:, k * quarter:(k + 1) * quarter], found)
        return found

    limit = jnp.zeros((elements, quarter), jnp.int32)
    full_limit = jnp.zeros((elements, width), jnp.int32)
    loads[0].wait()
    for e in range(elements):
        step = degree[e] + 1
        count = step * step * step * MODES // 64
        limit = jnp.where(row == e, count, limit)
        full_limit = jnp.where(full_row == e, count, full_limit)
    mask = (mode < limit).astype(jnp.float32)
    full_mask = (full_col % MODES < full_limit).astype(jnp.float32)
    loads[1].wait()
    src_half = (source[...] * mask).astype(jnp.bfloat16).astype(jnp.float32)
    src_buf[blk, :, :quarter] = src_half

    for load in loads[2:7]:
        load.wait()
    owner = [face_elem[f] for f in range(faces)]
    target = []
    for f in range(faces):
        side = face_side[f]
        slot = side
        for s, wanted in enumerate(side_slot):
            if wanted != s:
                slot = jnp.where(side == s, wanted, slot)
        target.append(slot * elements + face_peer[f])

    pick_row = lax.broadcasted_iota(jnp.int32, (elements, table), 0)
    pick_col = lax.broadcasted_iota(jnp.int32, (elements, table), 1)
    pick = jnp.concatenate(
        [
            jnp.where((pick_row == owner[f]) & (pick_col == target[f]), 1.0, 0.0)
            for f in range(faces)
        ],
        axis=0,
    ).astype(jnp.bfloat16)
    group = max(1, 256 // quarter)
    starts = list(range(0, faces, group))
    spread_row = lax.broadcasted_iota(jnp.int32, (table, group * elements), 0)
    spread_col = lax.broadcasted_iota(jnp.int32, (table, group * elements), 1)
    place_of = []
    for first in starts:
        hot = jnp.zeros((table, group * elements), jnp.float32)
        for f in range(first, min(first + group, faces)):
            col = (f - first) * elements + owner[f]
            hot = jnp.where((spread_row == target[f]) & (spread_col == col), 1.0, hot)
        place_of.append(hot)
    place_of = jnp.concatenate(place_of, axis=0).astype(jnp.bfloat16)
    group_col = lax.broadcasted_iota(jnp.int32, (elements, group * quarter), 1)
    table_lane = lax.broadcasted_iota(jnp.int32, (table, LANES), 1)
    chunk = math.gcd(faces, max(1, LANES // elements))
    chunk_lane = lax.broadcasted_iota(jnp.int32, (quarter, chunk * elements), 1)
    fold_row = lax.broadcasted_iota(jnp.int32, (elements, 2 * chunk * elements), 0)
    fold_col = lax.broadcasted_iota(jnp.int32, (elements, 2 * chunk * elements), 1)
    fold = jnp.where(fold_col % elements == fold_row, 1.0, 0.0).astype(jnp.bfloat16)

    pl.semaphore_wait(barrier, slots * blocks - 1)
    to_siblings(src_buf, src_sem)

    weight = residual[...] * mask
    high = weight.astype(jnp.bfloat16).astype(jnp.float32)
    low = weight - high
    row16 = lax.broadcasted_iota(jnp.int32, (2 * elements, quarter), 0)
    both = jnp.concatenate([high, low], axis=0)
    loads[7].wait()
    dual = jnp.zeros((2 * elements, width), jnp.float32)
    for e in range(elements):
        left = jnp.where((row16 == e) | (row16 == e + elements), both, 0.0).astype(jnp.bfloat16)
        dual += jnp.dot(left, inv_off[e], preferred_element_type=jnp.float32)
    dual = dual[:elements] + dual[elements:]
    dual_buf[blk, :, :width] = dual + in_place(weight * inv_diag[...])

    def invert(own, full):
        total = inv_diag[...] * own
        for e in range(elements):
            left = jnp.where(full_row == e, full, 0.0).astype(jnp.bfloat16)
            total += lax.dot_general(left, inv_off[e], NT, preferred_element_type=jnp.float32)
        return total

    finish(src_buf, blocks - 1, src_sem.at[1])
    base = invert(src_half, joined(src_buf, elements)) * mask
    dual_buf[blk, :, width:] = jnp.broadcast_to(
        jnp.sum(weight * base, axis=1, keepdims=True), (elements, dual_buf.shape[2] - width)
    )
    loads[8].wait()

    def one_sweep(sweep, carry):
        adjoint, _ = carry
        state, sent, back, coup = (
            buf.at[sweep] for buf in (state_buf, sent_buf, back_buf, coup_buf)
        )
        state_sems, back_sems, coup_sems = (
            sems.at[sweep] for sems in (state_sem, back_sem, coup_sem)
        )
        own_state = adjoint.astype(jnp.bfloat16).astype(jnp.float32)
        block = jnp.concatenate(
            [own_state, jnp.zeros((elements, LANES - quarter), jnp.float32)], axis=1
        )
        turned_block = block
        for k in range(1, blocks):
            turned_block = jnp.where(
                blk == k, pltpu.roll(block, k * quarter % LANES, 1), turned_block
            )
        state[blk] = turned_block.astype(jnp.bfloat16)
        for slot in far_first:
            for k in range(blocks):
                send(state.at[blk], state.at[slot * blocks + blk], state_sems, away(slot, -1), k)
        to_siblings(state, state_sems)

        repeated = jnp.concatenate([own_state] * group, axis=1)
        stacked = jnp.concatenate(
            [
                jnp.where(
                    (group_col >= g * quarter) & (group_col < (g + 1) * quarter), repeated, 0.0
                )
                for g in range(group)
            ],
            axis=0,
        ).astype(jnp.bfloat16)
        lefts = jnp.dot(place_of, stacked, preferred_element_type=jnp.float32)
        turned = jnp.zeros((table, width), jnp.float32)
        for index, first in enumerate(starts):
            last = min(first + group, faces)
            depth = (last - first) * quarter
            left = lefts[index * table:(index + 1) * table, :depth].astype(jnp.bfloat16)
            turned += jnp.dot(
                left, coupling[first:last].reshape(depth, width),
                preferred_element_type=jnp.float32,
            )
        sent[:, :, :width] = turned.reshape(slots, elements, width).astype(jnp.bfloat16)
        for slot in far_first:
            send(sent.at[slot], back.at[slot], back_sems, away(slot, 1), blk)

        finish(state, slots * blocks - 1, state_sems.at[1])
        columns = [
            jnp.concatenate(
                [state[slot * blocks + k].astype(jnp.float32) for slot in range(slots)], axis=0
            )
            for k in range(blocks)
        ]
        tiles = []
        for start in range(0, width, LANES):
            inside = [k for k in range(blocks)
                      if k * quarter < start + LANES and (k + 1) * quarter > start]
            joint = columns[inside[-1]]
            for k in inside[-2::-1]:
                joint = jnp.where(table_lane < (k + 1) * quarter - start, columns[k], joint)
            tiles.append(joint)
        every = jnp.concatenate(tiles, axis=1)[:, :width].astype(jnp.bfloat16)
        picked = jnp.dot(pick, every, preferred_element_type=jnp.float32).astype(jnp.bfloat16)
        held = jnp.zeros((quarter, chunk * elements), jnp.float32)
        for first in range(0, faces, chunk):
            product = lax.dot_general(
                coupling[first:first + chunk].reshape(chunk * quarter, width),
                picked[first * elements:(first + chunk) * elements],
                NT,
                preferred_element_type=jnp.float32,
            )
            for f in range(chunk):
                chosen = (chunk_lane >= f * elements) & (chunk_lane < (f + 1) * elements)
                held += jnp.where(chosen, product[f * quarter:(f + 1) * quarter], 0.0)
        high = held.astype(jnp.bfloat16)
        low = (held - high.astype(jnp.float32)).astype(jnp.bfloat16)
        own_terms = lax.dot_general(
            fold, jnp.concatenate([high, low], axis=1), NT, preferred_element_type=jnp.float32
        )
        partial = turned[:elements] + in_place(own_terms)

        finish(back, slots - 1, back_sems.at[1])
        for slot in range(1, slots):
            partial += back[slot].astype(jnp.float32)[:, :width]
        coup[blk, :, :width] = partial
        to_siblings(coup, coup_sems)
        finish(coup, blocks - 1, coup_sems.at[1])
        coupled = coup[0]
        for k in range(1, blocks):
            coupled += coup[k]
        full = (coupled[:, :width] * full_mask).astype(jnp.bfloat16).astype(jnp.float32)
        return (base - invert(own_part(full), full)) * mask, full

    to_siblings(dual_buf, dual_sem)
    adjoint, full = lax.fori_loop(
        0, SWEEPS, one_sweep, (base, jnp.zeros((elements, width), jnp.float32))
    )

    result_out[:elements, :quarter] = adjoint
    finish(dual_buf, blocks - 1, dual_sem.at[1])
    dual = dual_buf[0]
    for k in range(1, blocks):
        dual += dual_buf[k]
    weights = dual[:, width:width + 1] - jnp.sum(dual[:, :width] * full, axis=1, keepdims=True)
    lane = lax.broadcasted_iota(jnp.int32, (elements, LANES), 1)
    sub = lax.broadcasted_iota(jnp.int32, (elements, LANES), 0)
    result_out[elements:elements + 1, :] = jnp.sum(
        jnp.where(lane == sub, weights, 0.0), axis=0, keepdims=True
    )

    finish(src_buf, blocks - 1, src_sem.at[0])
    finish(dual_buf, blocks - 1, dual_sem.at[0])
    for sweep in range(SWEEPS):
        finish(state_buf.at[sweep], slots * blocks - 1, state_sem.at[sweep, 0])
        finish(back_buf.at[sweep], slots - 1, back_sem.at[sweep, 0])
        finish(coup_buf.at[sweep], blocks - 1, coup_sem.at[sweep, 0])


def split_result(result, adjoint, indicator):
    elements, quarter = adjoint.shape
    adjoint[...] = result[:elements, :quarter]
    indicator[...] = result[elements:elements + 1, :elements]


def local(degree, face_elem, face_side, face_peer, coupling, inv_diag, inv_off, source, residual):
    elements, quarter = source.shape
    parts, blocks = lax.axis_size("dom"), lax.axis_size("blk")
    width = coupling.shape[2]
    slots = len(slots_of(parts)[0])
    vmem = pl.BlockSpec(memory_space=pltpu.VMEM)
    hbm = pl.BlockSpec(memory_space=pl.ANY)
    tile = (elements, LANES)
    dual_width = (width // LANES + 1) * LANES
    full_width = -(-width // LANES) * LANES
    dma = pltpu.SemaphoreType.DMA
    args = (degree, face_elem, face_side, face_peer, coupling, inv_diag, inv_off, source, residual)
    result = pl.pallas_call(
        functools.partial(kernel, parts, blocks),
        out_shape=jax.ShapeDtypeStruct((2 * elements, LANES), jnp.float32),
        in_specs=[hbm] * len(args),
        out_specs=vmem,
        scratch_shapes=[pltpu.SMEM(arg.shape, arg.dtype) for arg in args[:4]]
        + [pltpu.VMEM(arg.shape, arg.dtype) for arg in args[4:]]
        + [
            pltpu.VMEM((blocks,) + tile, jnp.float32),
            pltpu.VMEM((SWEEPS, slots * blocks) + tile, jnp.bfloat16),
            pltpu.VMEM((SWEEPS, slots, elements, full_width), jnp.bfloat16),
            pltpu.VMEM((SWEEPS, slots, elements, full_width), jnp.bfloat16),
            pltpu.VMEM((SWEEPS, blocks, elements, full_width), jnp.float32),
            pltpu.VMEM((blocks, elements, dual_width), jnp.float32),
            dma((len(args),)), dma((2,)), dma((2,)),
        ]
        + [dma((SWEEPS, 2))] * 3,
        compiler_params=pltpu.CompilerParams(
            collective_id=0, has_side_effects=True, vmem_limit_bytes=60 * 2**20
        ),
    )(*args)
    adjoint, indicator = pl.pallas_call(
        split_result,
        out_shape=(
            jax.ShapeDtypeStruct((elements, quarter), jnp.float32),
            jax.ShapeDtypeStruct((1, elements), jnp.float32),
        ),
        in_specs=[vmem],
        out_specs=(vmem, vmem),
        compiler_params=pltpu.CompilerParams(vmem_limit_bytes=60 * 2**20),
    )(result)
    return adjoint, indicator.reshape(elements)


def solution(mesh):
    in_specs = (
        P("dom"),
        P("dom"),
        P("dom"),
        P("dom"),
        P("dom", "blk", None),
        P("dom", "blk"),
        P("dom", "blk", None),
        P("dom", "blk"),
        P("dom", "blk"),
    )
    out_specs = (P("dom", "blk"), P("dom"))
    return jax.shard_map(local, mesh=mesh, in_specs=in_specs, out_specs=out_specs, check_vma=False)
```

```python
import functools
import math

import jax
import jax.numpy as jnp
from jax import lax
from jax.experimental import pallas as pl
from jax.experimental.pallas import tpu as pltpu
from jax.sharding import PartitionSpec as P

MODES = 64
SWEEPS = 2
NEIGH = 8
LANES = 128
MESH = pl.DeviceIdType.MESH
NT = (((1,), (1,)), ((), ()))


def slots_of(parts):
    half = NEIGH // 2
    offsets = [0] + list(range(1, half + 1)) + [-k for k in range(1, half + 1)]
    unique, side_slot = [], []
    for offset in offsets:
        wrapped = offset % parts
        if wrapped not in unique:
            unique.append(wrapped)
        side_slot.append(unique.index(wrapped))
    return unique, side_slot


def kernel(
    parts, blocks,
    degree_hbm, elem_hbm, side_hbm, peer_hbm, coupling_hbm, diag_hbm, inv_off_hbm, source_hbm,
    residual_hbm,
    result_out,
    degree, face_elem, face_side, face_peer, coupling, inv_diag, inv_off, source, residual,
    src_buf, state_buf, sent_buf, back_buf, coup_buf, dual_buf,
    load_sem, src_sem, dual_sem, state_sem, back_sem, coup_sem,
):
    unique, side_slot = slots_of(parts)
    slots = len(unique)
    elements, quarter = source.shape
    faces, _, width = coupling.shape
    table = slots * elements
    dom = lax.axis_index("dom")
    blk = lax.axis_index("blk")

    loads = [
        pltpu.make_async_copy(src, dst, load_sem.at[place])
        for place, (src, dst) in enumerate([
            (degree_hbm, degree), (source_hbm, source), (elem_hbm, face_elem),
            (side_hbm, face_side), (peer_hbm, face_peer), (diag_hbm, inv_diag),
            (residual_hbm, residual), (inv_off_hbm, inv_off), (coupling_hbm, coupling),
        ])
    ]
    for load in loads:
        load.start()

    siblings = [lax.rem(blk + step, blocks) for step in range(1, blocks)]

    def away(slot, sign):
        return lax.rem(dom + (sign * unique[slot]) % parts, parts)

    barrier = pltpu.get_barrier_semaphore()
    for slot in range(1, slots):
        for k in range(blocks):
            pl.semaphore_signal(
                barrier, inc=1, device_id=(away(slot, 1), k), device_id_type=MESH
            )
    for k in siblings:
        pl.semaphore_signal(barrier, inc=1, device_id=(dom, k), device_id_type=MESH)

    def send(src, dst, sems, there, k):
        pltpu.make_async_remote_copy(
            src_ref=src, dst_ref=dst, send_sem=sems.at[0], recv_sem=sems.at[1],
            device_id=(there, k), device_id_type=MESH,
        ).start()

    def finish(buf, count, sem):
        part = buf.at[pl.ds(0, count)]
        pltpu.make_async_copy(part, part, sem).wait()

    def to_siblings(buf, sems):
        for k in siblings:
            send(buf.at[blk], buf.at[blk], sems, dom, k)

    def joined(buf, rows):
        return jnp.concatenate(
            [buf[k][:rows, :quarter].astype(jnp.float32) for k in range(blocks)], axis=1
        )

    row = lax.broadcasted_iota(jnp.int32, (elements, quarter), 0)
    mode = (lax.broadcasted_iota(jnp.int32, (elements, quarter), 1) + blk * quarter) % MODES
    full_row = lax.broadcasted_iota(jnp.int32, (elements, width), 0)
    full_col = lax.broadcasted_iota(jnp.int32, (elements, width), 1)
    mine = (full_col >= blk * quarter) & (full_col < (blk + 1) * quarter)

    def in_place(values):
        return jnp.where(mine, jnp.concatenate([values] * blocks, axis=1), 0.0)

    def own_part(values):
        found = values[:, :quarter]
        for k in range(1, blocks):
            found = jnp.where(blk == k, values[:, k * quarter:(k + 1) * quarter], found)
        return found

    limit = jnp.zeros((elements, quarter), jnp.int32)
    full_limit = jnp.zeros((elements, width), jnp.int32)
    loads[0].wait()
    for e in range(elements):
        step = degree[e] + 1
        count = step * step * step * MODES // 64
        limit = jnp.where(row == e, count, limit)
        full_limit = jnp.where(full_row == e, count, full_limit)
    mask = (mode < limit).astype(jnp.float32)
    full_mask = (full_col % MODES < full_limit).astype(jnp.float32)
    loads[1].wait()
    src_half = (source[...] * mask).astype(jnp.bfloat16).astype(jnp.float32)
    src_buf[blk, :, :quarter] = src_half

    for load in loads[2:7]:
        load.wait()
    owner = [face_elem[f] for f in range(faces)]
    target = []
    for f in range(faces):
        side = face_side[f]
        slot = side
        for s, wanted in enumerate(side_slot):
            if wanted != s:
                slot = jnp.where(side == s, wanted, slot)
        target.append(slot * elements + face_peer[f])

    pick_row = lax.broadcasted_iota(jnp.int32, (elements, table), 0)
    pick_col = lax.broadcasted_iota(jnp.int32, (elements, table), 1)
    pick = jnp.concatenate(
        [
            jnp.where((pick_row == owner[f]) & (pick_col == target[f]), 1.0, 0.0)
            for f in range(faces)
        ],
        axis=0,
    ).astype(jnp.bfloat16)
    group = max(1, 256 // quarter)
    starts = list(range(0, faces, group))
    spread_row = lax.broadcasted_iota(jnp.int32, (table, group * elements), 0)
    spread_col = lax.broadcasted_iota(jnp.int32, (table, group * elements), 1)
    place_of = []
    for first in starts:
        hot = jnp.zeros((table, group * elements), jnp.float32)
        for f in range(first, min(first + group, faces)):
            col = (f - first) * elements + owner[f]
            hot = jnp.where((spread_row == target[f]) & (spread_col == col), 1.0, hot)
        place_of.append(hot)
    place_of = jnp.concatenate(place_of, axis=0).astype(jnp.bfloat16)
    group_col = lax.broadcasted_iota(jnp.int32, (elements, group * quarter), 1)
    chunk = math.gcd(faces, max(1, LANES // elements))
    chunk_lane = lax.broadcasted_iota(jnp.int32, (quarter, chunk * elements), 1)
    fold_row = lax.broadcasted_iota(jnp.int32, (elements, 2 * chunk * elements), 0)
    fold_col = lax.broadcasted_iota(jnp.int32, (elements, 2 * chunk * elements), 1)
    fold = jnp.where(fold_col % elements == fold_row, 1.0, 0.0).astype(jnp.bfloat16)

    pl.semaphore_wait(barrier, slots * blocks - 1)
    to_siblings(src_buf, src_sem)

    weight = residual[...] * mask
    high = weight.astype(jnp.bfloat16).astype(jnp.float32)
    low = weight - high
    row16 = lax.broadcasted_iota(jnp.int32, (2 * elements, quarter), 0)
    both = jnp.concatenate([high, low], axis=0)
    loads[7].wait()
    dual = jnp.zeros((2 * elements, width), jnp.float32)
    for e in range(elements):
        left = jnp.where((row16 == e) | (row16 == e + elements), both, 0.0).astype(jnp.bfloat16)
        dual += jnp.dot(left, inv_off[e], preferred_element_type=jnp.float32)
    dual = dual[:elements] + dual[elements:]
    dual_buf[blk, :, :width] = dual + in_place(weight * inv_diag[...])

    def invert(own, full):
        total = inv_diag[...] * own
        for e in range(elements):
            left = jnp.where(full_row == e, full, 0.0).astype(jnp.bfloat16)
            total += lax.dot_general(left, inv_off[e], NT, preferred_element_type=jnp.float32)
        return total

    finish(src_buf, blocks - 1, src_sem.at[1])
    base = invert(src_half, joined(src_buf, elements)) * mask
    loads[8].wait()

    def one_sweep(sweep, carry):
        adjoint, _ = carry
        state, sent, back, coup = (
            buf.at[sweep] for buf in (state_buf, sent_buf, back_buf, coup_buf)
        )
        state_sems, back_sems, coup_sems = (
            sems.at[sweep] for sems in (state_sem, back_sem, coup_sem)
        )
        own_state = adjoint.astype(jnp.bfloat16).astype(jnp.float32)
        state[blk] = jnp.concatenate(
            [own_state, jnp.zeros((elements, LANES - quarter), jnp.float32)], axis=1
        ).astype(jnp.bfloat16)
        for slot in range(1, slots):
            for k in range(blocks):
                send(state.at[blk], state.at[slot * blocks + blk], state_sems, away(slot, -1), k)
        to_siblings(state, state_sems)

        repeated = jnp.concatenate([own_state] * group, axis=1)
        stacked = jnp.concatenate(
            [
                jnp.where(
                    (group_col >= g * quarter) & (group_col < (g + 1) * quarter), repeated, 0.0
                )
                for g in range(group)
            ],
            axis=0,
        ).astype(jnp.bfloat16)
        lefts = jnp.dot(place_of, stacked, preferred_element_type=jnp.float32)
        turned = jnp.zeros((table, width), jnp.float32)
        for index, first in enumerate(starts):
            last = min(first + group, faces)
            depth = (last - first) * quarter
            left = lefts[index * table:(index + 1) * table, :depth].astype(jnp.bfloat16)
            turned += jnp.dot(
                left, coupling[first:last].reshape(depth, width),
                preferred_element_type=jnp.float32,
            )
        sent[:, :, :width] = turned.reshape(slots, elements, width).astype(jnp.bfloat16)
        for slot in range(1, slots):
            send(sent.at[slot], back.at[slot], back_sems, away(slot, 1), blk)

        @pl.when(sweep == 0)
        def send_dual():
            dual_buf[blk, :, width:] = jnp.broadcast_to(
                jnp.sum(weight * base, axis=1, keepdims=True),
                (elements, dual_buf.shape[2] - width),
            )
            to_siblings(dual_buf, dual_sem)

        finish(state, slots * blocks - 1, state_sems.at[1])
        every = jnp.concatenate(
            [
                jnp.concatenate(
                    [
                        state[slot * blocks + k].astype(jnp.float32)[:, :quarter]
                        for k in range(blocks)
                    ],
                    axis=1,
                )
                for slot in range(slots)
            ],
            axis=0,
        ).astype(jnp.bfloat16)
        picked = jnp.dot(pick, every, preferred_element_type=jnp.float32).astype(jnp.bfloat16)
        held = jnp.zeros((quarter, chunk * elements), jnp.float32)
        for first in range(0, faces, chunk):
            product = lax.dot_general(
                coupling[first:first + chunk].reshape(chunk * quarter, width),
                picked[first * elements:(first + chunk) * elements],
                NT,
                preferred_element_type=jnp.float32,
            )
            for f in range(chunk):
                chosen = (chunk_lane >= f * elements) & (chunk_lane < (f + 1) * elements)
                held += jnp.where(chosen, product[f * quarter:(f + 1) * quarter], 0.0)
        high = held.astype(jnp.bfloat16)
        low = (held - high.astype(jnp.float32)).astype(jnp.bfloat16)
        own_terms = lax.dot_general(
            fold, jnp.concatenate([high, low], axis=1), NT, preferred_element_type=jnp.float32
        )
        partial = turned[:elements] + in_place(own_terms)

        finish(back, slots - 1, back_sems.at[1])
        for slot in range(1, slots):
            partial += back[slot].astype(jnp.float32)[:, :width]
        coup[blk, :, :width] = partial
        to_siblings(coup, coup_sems)
        finish(coup, blocks - 1, coup_sems.at[1])
        coupled = coup[0]
        for k in range(1, blocks):
            coupled += coup[k]
        full = (coupled[:, :width] * full_mask).astype(jnp.bfloat16).astype(jnp.float32)
        return (base - invert(own_part(full), full)) * mask, full

    adjoint, full = lax.fori_loop(
        0, SWEEPS, one_sweep, (base, jnp.zeros((elements, width), jnp.float32))
    )

    result_out[:elements, :quarter] = adjoint
    finish(dual_buf, blocks - 1, dual_sem.at[1])
    dual = dual_buf[0]
    for k in range(1, blocks):
        dual += dual_buf[k]
    weights = dual[:, width:width + 1] - jnp.sum(dual[:, :width] * full, axis=1, keepdims=True)
    lane = lax.broadcasted_iota(jnp.int32, (elements, LANES), 1)
    sub = lax.broadcasted_iota(jnp.int32, (elements, LANES), 0)
    result_out[elements:elements + 1, :] = jnp.sum(
        jnp.where(lane == sub, weights, 0.0), axis=0, keepdims=True
    )

    finish(src_buf, blocks - 1, src_sem.at[0])
    finish(dual_buf, blocks - 1, dual_sem.at[0])
    for sweep in range(SWEEPS):
        finish(state_buf.at[sweep], slots * blocks - 1, state_sem.at[sweep, 0])
        finish(back_buf.at[sweep], slots - 1, back_sem.at[sweep, 0])
        finish(coup_buf.at[sweep], blocks - 1, coup_sem.at[sweep, 0])


def split_result(result, adjoint, indicator):
    elements, quarter = adjoint.shape
    adjoint[...] = result[:elements, :quarter]
    indicator[...] = result[elements:elements + 1, :elements]


def local(degree, face_elem, face_side, face_peer, coupling, inv_diag, inv_off, source, residual):
    elements, quarter = source.shape
    parts, blocks = lax.axis_size("dom"), lax.axis_size("blk")
    width = coupling.shape[2]
    slots = len(slots_of(parts)[0])
    vmem = pl.BlockSpec(memory_space=pltpu.VMEM)
    hbm = pl.BlockSpec(memory_space=pl.ANY)
    tile = (elements, LANES)
    dual_width = (width // LANES + 1) * LANES
    full_width = -(-width // LANES) * LANES
    dma = pltpu.SemaphoreType.DMA
    args = (degree, face_elem, face_side, face_peer, coupling, inv_diag, inv_off, source, residual)
    result = pl.pallas_call(
        functools.partial(kernel, parts, blocks),
        out_shape=jax.ShapeDtypeStruct((2 * elements, LANES), jnp.float32),
        in_specs=[hbm] * len(args),
        out_specs=vmem,
        scratch_shapes=[pltpu.SMEM(arg.shape, arg.dtype) for arg in args[:4]]
        + [pltpu.VMEM(arg.shape, arg.dtype) for arg in args[4:]]
        + [
            pltpu.VMEM((blocks,) + tile, jnp.float32),
            pltpu.VMEM((SWEEPS, slots * blocks) + tile, jnp.bfloat16),
            pltpu.VMEM((SWEEPS, slots, elements, full_width), jnp.bfloat16),
            pltpu.VMEM((SWEEPS, slots, elements, full_width), jnp.bfloat16),
            pltpu.VMEM((SWEEPS, blocks, elements, full_width), jnp.float32),
            pltpu.VMEM((blocks, elements, dual_width), jnp.float32),
            dma((len(args),)), dma((2,)), dma((2,)),
        ]
        + [dma((SWEEPS, 2))] * 3,
        compiler_params=pltpu.CompilerParams(
            collective_id=0, has_side_effects=True, vmem_limit_bytes=60 * 2**20
        ),
    )(*args)
    adjoint, indicator = pl.pallas_call(
        split_result,
        out_shape=(
            jax.ShapeDtypeStruct((elements, quarter), jnp.float32),
            jax.ShapeDtypeStruct((1, elements), jnp.float32),
        ),
        in_specs=[vmem],
        out_specs=(vmem, vmem),
        compiler_params=pltpu.CompilerParams(vmem_limit_bytes=60 * 2**20),
    )(result)
    return adjoint, indicator.reshape(elements)


def solution(mesh):
    in_specs = (
        P("dom"),
        P("dom"),
        P("dom"),
        P("dom"),
        P("dom", "blk", None),
        P("dom", "blk"),
        P("dom", "blk", None),
        P("dom", "blk"),
        P("dom", "blk"),
    )
    out_specs = (P("dom", "blk"), P("dom"))
    return jax.shard_map(local, mesh=mesh, in_specs=in_specs, out_specs=out_specs, check_vma=False)
```
